512 devices in a mesh: row: 2 (over core), nbr: 16 (over z_lo, y), feat: 16 (over x, z_hi).
Axes of the slice: x: 4, y: 4, z: 16 (z_hi: 4, z_lo: 4; z = z_hi * 4 + z_lo), core: 2. Of those that a mesh axis runs over, the one named last changes fastest.
Arguments:
- features: float32 [1024, 32768], P('feat', 'nbr'), may hold values from -6 to 6
- tile_list: int32 [2, 16, 2, 256], P('row', 'nbr'), may hold values from 0 to 15, as said below
- tile_count: int32 [2, 16], P('row', 'nbr'), may hold values from 96 to 256
- weight: float32 [1024, 1024], P(('row', 'nbr'), 'feat'), may hold values from -0.1875 to 0.1875
- cotangent: float32 [4096, 1024], P(('row', 'nbr'), 'feat'), may hold values from -6 to 6
Outputs:
- activations: float32 [4096, 1024], P(('row', 'nbr'), 'feat')
- feature_grad: float32 [1024, 32768], P('feat', 'nbr')
- weight_grad: float32 [1024, 1024], P(('row', 'nbr'), 'feat')
The draws below stay inside these ranges and needn't reach their ends.
Inputs may be any that keep to these rules, and one draw needn't show every extreme that they name: `tile_list`: each device's list names every (row block, column block) pair of its block exactly once; only the first tile_count entries are used.
All inputs are finite; a program needn't handle non-finite values.
Results may differ from the reference program's by a relative error of at most 0.0003.
Values sent between devices are 32-bit elements; how exact they have to be, the bound alone decides.
No kernel may reach another device: no remote copies, remote signals or barrier semaphores. Data moves between devices by JAX's collectives and lax.ppermute only.
A program may use at most 64 MiB of HBM per device.

```python
import jax
import jax.numpy as jnp
from jax import lax

F = 1024
TILE = 128
R_DEV = 2048
C_DEV = 2048
TILE_MAX = 256
TILE_MIN = 96
ROWS = 4096
COLS = 32768
N_ROW = 2
N_NBR = 16


def draw_tile_count(key, part):
    key = jax.random.fold_in(key, 1)
    spread = max(TILE_MAX - TILE_MIN, 1)
    uniform_pick = jax.random.randint(key, (N_ROW, N_NBR), 0, TILE_MAX - TILE_MIN + 1)
    skewed = uniform_pick * uniform_pick // spread * uniform_pick // spread
    counts = TILE_MIN + skewed
    counts = counts.at[0, 0].set(TILE_MAX).at[1, 0].set(TILE_MIN)
    return counts.astype(jnp.int32)


def draw_tile_list(key, part):
    key = jax.random.fold_in(key, 2)
    device_keys = jax.random.split(key, N_ROW * N_NBR)

    def shuffled(single_key):
        return jax.random.permutation(single_key, TILE_MAX)
    orders = jax.vmap(shuffled)(device_keys).astype(jnp.int32)
    col_blocks = C_DEV // TILE
    stacked = jnp.stack([orders // col_blocks, orders % col_blocks], axis=1)
    return stacked.reshape(N_ROW, N_NBR, 2, TILE_MAX).astype(jnp.int32)


def shard_levels(key, shape, cuts, least, largest):
    factor_of, own = 1.0, jax.random.fold_in(key, 6)
    for dim, shards_of in cuts:
        steps = jnp.exp(jax.random.uniform(jax.random.fold_in(own, dim), (shards_of,), jnp.float32, least / len(cuts), largest / len(cuts)))
        factor_of = factor_of * jnp.repeat(steps, shape[dim] // shards_of).reshape([-1 if axis == dim else 1 for axis in range(len(shape))])
    return factor_of


def scatter_about(stream_key, extent, width, reach, pieces=(), held_as=jnp.bfloat16):
    factor_of = shard_levels(stream_key, extent, pieces, -0.22, 0.18) if pieces else 1.0
    values = jax.random.normal(stream_key, extent, jnp.float32) * width * factor_of
    return jnp.minimum(jnp.maximum(values, -reach), reach).astype(held_as)


def setup_inputs(seed: int = 0) -> dict:
    key_of = jax.random.split(jax.random.key(seed), 6)
    return {
        "features": scatter_about(key_of[0], (F, COLS), 1.0, 6.0, ((0, 16), (1, 16)), jnp.float32),
        "tile_list": draw_tile_list(jax.random.fold_in(key_of[5], 71), 0),
        "tile_count": draw_tile_count(jax.random.fold_in(key_of[5], 71), 0),
        "weight": scatter_about(key_of[3], (F, F), F ** -0.5, 0.1875, ((0, 32), (1, 16)), jnp.float32),
        "cotangent": scatter_about(key_of[4], (ROWS, F), 1.0, 6.0, ((0, 32), (1, 16)), jnp.float32),
    }


modulus = 32749
highest = lax.Precision.HIGHEST


def edge_value(row_index, col_index):
    hashed = ((row_index * row_index) % modulus * 3 + (col_index * col_index) % modulus * 5
              + (row_index * col_index) % modulus * 7 + row_index * 11 + col_index * 13) % modulus
    return hashed.astype(jnp.float32) / modulus - 0.5


def dense_block(tile_pairs, tile_total, row_id, nbr_id, edge_scale):
    slots = jnp.arange(TILE_MAX, dtype=jnp.int32)
    in_range = (slots < tile_total).astype(jnp.float32)
    row_onehot = (tile_pairs[0][:, None] == jnp.arange(R_DEV // TILE, dtype=jnp.int32)[None, :]).astype(jnp.float32) * in_range[:, None]
    col_onehot = (tile_pairs[1][:, None] == jnp.arange(C_DEV // TILE, dtype=jnp.int32)[None, :]).astype(jnp.float32)
    occupied = jnp.dot(row_onehot.T, col_onehot)
    occupied = jnp.repeat(jnp.repeat(occupied, TILE, axis=0), TILE, axis=1)
    rows_global = row_id * R_DEV + jnp.arange(R_DEV, dtype=jnp.int32)[:, None]
    cols_global = nbr_id * C_DEV + jnp.arange(C_DEV, dtype=jnp.int32)[None, :]
    return edge_value(rows_global, cols_global) * edge_scale * occupied


def reference(features, tile_list, tile_count, weight, cotangent):
    edge_scale = (12.0 / (C_DEV * N_NBR / 2)) ** 0.5
    blocks = features.T.reshape(N_NBR, C_DEV, F)
    nbr_ids = jnp.arange(N_NBR, dtype=jnp.int32)
    hidden_parts = []
    for row_id in range(N_ROW):
        def accumulate(running, items):
            nbr_id, block_x, pairs, totals = items
            adjacency = dense_block(pairs, totals, row_id, nbr_id, edge_scale)
            return running + jnp.dot(adjacency, block_x, precision=highest), None
        hidden_row, unused = lax.scan(accumulate, jnp.zeros((R_DEV, F), jnp.float32),
                                      (nbr_ids, blocks, tile_list[row_id], tile_count[row_id]))
        hidden_parts.append(hidden_row)
    hidden = jnp.concatenate(hidden_parts, axis=0)
    pre_act = jnp.dot(hidden, weight, precision=highest)
    squash = jax.nn.sigmoid(pre_act)
    activations = pre_act * squash
    grad_pre = cotangent * squash * (1.0 + pre_act * (1.0 - squash))
    grad_hidden = jnp.dot(grad_pre, weight.T, precision=highest)
    weight_grad = jnp.dot(hidden.T, grad_pre, precision=highest)
    grad_rows = grad_hidden.reshape(N_ROW, R_DEV, F)

    def column_block(carried, items):
        nbr_id, pairs, totals = items
        running = jnp.zeros((C_DEV, F), jnp.float32)
        for row_id in range(N_ROW):
            adjacency = dense_block(pairs[row_id], totals[row_id], row_id, nbr_id, edge_scale)
            running = running + jnp.dot(adjacency.T, grad_rows[row_id], precision=highest)
        return carried, running

    carried, stacked = lax.scan(column_block, jnp.zeros((), jnp.float32),
                                (nbr_ids, jnp.moveaxis(tile_list, 1, 0), tile_count.T))
    feature_grad = stacked.reshape(N_NBR * C_DEV, F).T
    return (activations, feature_grad, weight_grad)
```

```python
import functools

import jax
import jax.numpy as jnp
from jax import lax
from jax.experimental import pallas as pl
from jax.experimental.pallas import tpu as pltpu
from jax.sharding import Mesh
from jax.sharding import PartitionSpec as P

TILE = 128
MODULUS = 32749
INVERSE = 1.0 / MODULUS
HALF_STEP = 0.5 / MODULUS
highest = lax.Precision.HIGHEST
f32, bf16, i32 = jnp.float32, jnp.bfloat16, jnp.int32


def residue(value):
    quotient = jnp.floor(value.astype(f32) * INVERSE).astype(i32)
    rest = value - quotient * MODULUS
    rest = jnp.where(rest < 0, rest + MODULUS, rest)
    return jnp.where(rest >= MODULUS, rest - MODULUS, rest)


def split(value):
    high = value.astype(bf16)
    return high, (value - high.astype(f32)).astype(bf16)


def product_kernel(
    lane_blocks, sub_blocks, swap, sub_poly, lane_poly, scale,
    base_ref, count_ref, pairs_ref, source_ref, out_ref,
    sub_table, step_table, lane_table, mask_table, source_parts,
):
    sub_base, lane_base = base_ref[0], base_ref[1]
    width = source_parts.shape[0] // 2
    n_sub = sub_blocks * TILE
    slots = pairs_ref.shape[1]
    major, minor = (pairs_ref[1:2, :], pairs_ref[0:1, :]) if swap else (pairs_ref[0:1, :], pairs_ref[1:2, :])
    code = major * sub_blocks + minor
    code = jnp.where(lax.broadcasted_iota(i32, (1, slots), 1) < count_ref[0], code, -1)
    tiles = lane_blocks * sub_blocks
    listed = (lax.broadcasted_iota(i32, (tiles, slots), 0) == code).astype(f32)
    mask_table[...] = jnp.broadcast_to(jnp.sum(listed, axis=1, keepdims=True), (tiles, TILE))

    sub = sub_base + lax.broadcasted_iota(i32, (n_sub, TILE), 0)
    sub_table[...] = residue(sub * residue(sub_poly[0] * sub + sub_poly[1])).astype(f32) * INVERSE
    for l in range(sub_blocks):
        columns = slice(l * TILE, (l + 1) * TILE)
        piece = source_ref[l] if len(source_ref.shape) == 3 else source_ref[:, columns]
        high, low = split(piece)
        source_parts[:width, columns] = high
        source_parts[width:, columns] = low

    def block(j, carry):
        first_lane = lane_base + j * TILE
        lane = first_lane + lax.broadcasted_iota(i32, (TILE, TILE), 1)
        k = lax.broadcasted_iota(i32, (TILE, TILE), 0)
        step_table[...] = residue(7 * k * lane).astype(f32) * INVERSE
        lane = first_lane + lax.broadcasted_iota(i32, (sub_blocks, TILE), 1)
        first = sub_base + TILE * lax.broadcasted_iota(i32, (sub_blocks, TILE), 0)
        inner = residue(lane_poly[0] * lane + lane_poly[1] + 7 * first)
        lane_table[...] = residue(lane * inner).astype(f32) * INVERSE - 0.5
        total = jnp.zeros((2 * width, 2 * TILE), f32)
        for l in range(0, sub_blocks, 2):
            halves = []
            for at in (l, l + 1):
                turn = sub_table[at * TILE:(at + 1) * TILE, :] + step_table[...] + lane_table[at:at + 1, :]
                edge = turn - jnp.floor(turn + (0.5 + HALF_STEP))
                edge = edge * mask_table[pl.ds(j * sub_blocks + at, 1), :]
                halves.append(jnp.concatenate(split(edge), axis=1))
            total += jnp.dot(
                source_parts[:, l * TILE:(l + 2) * TILE], jnp.concatenate(halves, axis=0),
                preferred_element_type=f32,
            )
        total = total[:, :TILE] + total[:, TILE:]
        result = (total[:width] + total[width:]) * scale
        if len(out_ref.shape) == 3:
            out_ref[j] = result
        else:
            out_ref[:, pl.ds(pl.multiple_of(j * TILE, TILE), TILE)] = result
        return carry

    lax.fori_loop(0, lane_blocks, block, 0)


def edge_product(base, count, pairs, source, lane_blocks, sub_blocks, swap, sub_poly, lane_poly, scale, stacked):
    width = source.shape[1] if source.ndim == 3 else source.shape[0]
    shape = (lane_blocks, width, TILE) if stacked else (width, lane_blocks * TILE)
    tiles = lane_blocks * sub_blocks
    return pl.pallas_call(
        functools.partial(product_kernel, lane_blocks, sub_blocks, swap, sub_poly, lane_poly, scale),
        out_shape=jax.ShapeDtypeStruct(shape, f32),
        in_specs=[
            pl.BlockSpec(memory_space=pltpu.SMEM),
            pl.BlockSpec(memory_space=pltpu.SMEM),
            pl.BlockSpec(memory_space=pltpu.VMEM),
            pl.BlockSpec(memory_space=pltpu.VMEM),
        ],
        out_specs=pl.BlockSpec(memory_space=pltpu.VMEM),
        scratch_shapes=[
            pltpu.VMEM((sub_blocks * TILE, TILE), f32),
            pltpu.VMEM((TILE, TILE), f32),
            pltpu.VMEM((sub_blocks, TILE), f32),
            pltpu.VMEM((tiles, TILE), f32),
            pltpu.VMEM((2 * width, sub_blocks * TILE), bf16),
        ],
        compiler_params=pltpu.CompilerParams(vmem_limit_bytes=24 << 20),
        cost_estimate=pl.CostEstimate(flops=8 << 30, bytes_accessed=1 << 21, transcendentals=0),
    )(base, count, pairs, source)


def dot(a, b, dims=((1,), (0,))):
    return lax.dot_general(a, b, (dims, ((), ())), precision=highest, preferred_element_type=f32)


def layer_kernel(
    n_x, n_zh, at_ref, hidden_ref, own_ref, other_ref, cot_ref,
    act_ref, grad_ref, own_terms_ref, other_terms_ref, weight,
):
    core, zh = at_ref[0], at_ref[1]
    half = own_ref.shape[0]
    rows, width = own_ref.shape[2], own_ref.shape[3]
    weight[pl.ds(core * half, half)] = own_ref[...]
    weight[pl.ds((1 - core) * half, half)] = other_ref[...]
    hidden = hidden_ref[...].T
    depth = hidden.shape[1]
    grads = []
    for z in range(n_zh):
        columns = weight[:, z].reshape(depth, width)
        pre = dot(hidden, columns)
        squash = 1.0 / (1.0 + jnp.exp(-pre))
        grad_pre = cot_ref[z] * squash * (1.0 + pre * (1.0 - squash))
        grads.append(grad_pre)

        @pl.when(zh == z)
        def _():
            act_ref[...] = pre * squash
            own = hidden_ref[pl.ds(pl.multiple_of(core * (depth // 2), 8), depth // 2), :]
            other = hidden_ref[pl.ds(pl.multiple_of((1 - core) * (depth // 2), 8), depth // 2), :]
            own_terms_ref[...] = dot(own, grad_pre).reshape(own_terms_ref.shape)
            other_terms_ref[...] = dot(other, grad_pre).reshape(other_terms_ref.shape)

    per_block = width // rows
    for x in range(n_x):
        total = None
        for z in range(n_zh):
            picked = weight[pl.ds((x * n_zh + zh) * per_block, per_block), z].reshape(width, width)
            term = dot(picked, grads[z], ((1,), (1,)))
            total = term if total is None else total + term
        grad_ref[x] = total


def layer(at, hidden_all, own, other, cot, n_x, n_zh):
    half, _, rows, width = own.shape
    n_rows = hidden_all.shape[1]
    terms = jax.ShapeDtypeStruct((half, rows, width), f32)
    vmem = pl.BlockSpec(memory_space=pltpu.VMEM)
    return pl.pallas_call(
        functools.partial(layer_kernel, n_x, n_zh),
        out_shape=(
            jax.ShapeDtypeStruct((n_rows, width), f32),
            jax.ShapeDtypeStruct((n_x, width, n_rows), f32),
            terms, terms,
        ),
        in_specs=[pl.BlockSpec(memory_space=pltpu.SMEM), vmem, vmem, vmem, vmem],
        out_specs=(vmem, vmem, vmem, vmem),
        scratch_shapes=[pltpu.VMEM((2 * half, n_zh, rows, width), f32)],
        compiler_params=pltpu.CompilerParams(vmem_limit_bytes=32 << 20),
        cost_estimate=pl.CostEstimate(flops=1 << 30, bytes_accessed=1 << 21, transcendentals=0),
    )(at, hidden_all, own, other, cot)


def spread(value, axes, n):
    return lax.all_to_all(jnp.broadcast_to(value[None], (n,) + value.shape), axes, 0, 0)


def per_device(features, tile_list, tile_count, weight, cotangent):
    nbr, feat = ("zl", "y"), ("x", "zh")
    pairs, count = tile_list[0, 0], tile_count[0]
    n_nbr = lax.axis_size(nbr)
    n_x, n_zh = lax.axis_size("x"), lax.axis_size("zh")
    core, nbr_id = lax.axis_index("core"), lax.axis_index(nbr)
    width, c_dev = features.shape
    n_rows = cotangent.shape[0]
    r_dev = n_rows * n_nbr
    scale = (12.0 / (c_dev * n_nbr / 2)) ** 0.5
    row_blocks, col_blocks = r_dev // TILE, c_dev // TILE
    swap_core = [(0, 1), (1, 0)]

    weight_z = spread(weight, "zh", n_zh)
    cot_z = spread(cotangent, "zh", n_zh)
    own = spread(weight_z, nbr, n_nbr)
    other = lax.ppermute(own, "core", swap_core)

    bases = jnp.stack([nbr_id * c_dev, core * r_dev]).astype(i32)
    partial = edge_product(bases, count, pairs, features, row_blocks, col_blocks, False, (5, 13), (3, 11), scale, True)
    hidden = jnp.sum(lax.all_to_all(partial, nbr, 0, 0), axis=0)
    hidden_all = lax.all_gather(hidden, "zh", axis=0, tiled=True)
    hidden_all = lax.all_gather(hidden_all, "x", axis=0, tiled=True)

    at = jnp.stack([core, lax.axis_index("zh")]).astype(i32)
    activations, grad_terms, own_terms, other_terms = layer(at, hidden_all, own, other, cot_z, n_x, n_zh)

    grad_hidden = jnp.sum(lax.all_to_all(grad_terms, "x", 0, 0), axis=0)
    grad_block = spread(grad_hidden, nbr, n_nbr)
    terms = own_terms + lax.ppermute(other_terms, "core", swap_core)
    weight_grad = jnp.sum(lax.all_to_all(terms, nbr, 0, 0), axis=0)

    column_part = edge_product(
        bases[::-1], count, pairs, grad_block, col_blocks, row_blocks, True, (3, 11), (5, 13), scale, False
    )
    feature_grad = column_part + lax.ppermute(column_part, "core", swap_core)
    return activations, feature_grad, weight_grad


def halves(n):
    minor = 1
    while minor * minor < n:
        minor *= 2
    return n // minor, minor


def solution(mesh):
    sizes = (mesh.shape["row"], *halves(mesh.shape["nbr"]), *halves(mesh.shape["feat"]))
    fine = Mesh(mesh.devices.reshape(sizes), ("core", "zl", "y", "x", "zh"))
    nbr, feat = ("zl", "y"), ("x", "zh")
    rows = ("core", *nbr)
    in_specs = (P(feat, nbr), P("core", nbr, None, None), P("core", nbr), P(rows, feat), P(rows, feat))
    out_specs = (P(rows, feat), P(feat, nbr), P(rows, feat))
    return jax.shard_map(per_device, mesh=fine, in_specs=in_specs, out_specs=out_specs, check_vma=False)
```

```python
import functools

import jax
import jax.numpy as jnp
from jax import lax
from jax.experimental import pallas as pl
from jax.experimental.pallas import tpu as pltpu
from jax.sharding import Mesh
from jax.sharding import PartitionSpec as P

TILE = 128
MODULUS = 32749
INVERSE = 1.0 / MODULUS
HALF_STEP = 0.5 / MODULUS
highest = lax.Precision.HIGHEST
f32, bf16, i32 = jnp.float32, jnp.bfloat16, jnp.int32


def residue(value):
    quotient = jnp.floor(value.astype(f32) * INVERSE).astype(i32)
    rest = value - quotient * MODULUS
    rest = jnp.where(rest < 0, rest + MODULUS, rest)
    return jnp.where(rest >= MODULUS, rest - MODULUS, rest)


def split(value):
    high = value.astype(bf16)
    return high, (value - high.astype(f32)).astype(bf16)


def product_kernel(
    lane_blocks, sub_blocks, swap, sub_poly, lane_poly, scale,
    base_ref, count_ref, pairs_ref, source_ref, out_ref,
    sub_table, step_table, lane_table, mask_table, source_parts,
):
    sub_base, lane_base = base_ref[0], base_ref[1]
    width = source_parts.shape[0] // 2
    n_sub = sub_blocks * TILE
    slots = pairs_ref.shape[1]
    major, minor = (pairs_ref[1:2, :], pairs_ref[0:1, :]) if swap else (pairs_ref[0:1, :], pairs_ref[1:2, :])
    code = major * sub_blocks + minor
    code = jnp.where(lax.broadcasted_iota(i32, (1, slots), 1) < count_ref[0], code, -1)
    tiles = lane_blocks * sub_blocks
    listed = (lax.broadcasted_iota(i32, (tiles, slots), 0) == code).astype(f32)
    mask_table[...] = jnp.broadcast_to(jnp.sum(listed, axis=1, keepdims=True), (tiles, TILE))

    sub = sub_base + lax.broadcasted_iota(i32, (n_sub, TILE), 0)
    sub_table[...] = residue(sub * residue(sub_poly[0] * sub + sub_poly[1])).astype(f32) * INVERSE
    for l in range(sub_blocks):
        columns = slice(l * TILE, (l + 1) * TILE)
        piece = source_ref[l] if len(source_ref.shape) == 3 else source_ref[:, columns]
        high, low = split(piece)
        source_parts[:width, columns] = high
        source_parts[width:, columns] = low

    def block(j, carry):
        first_lane = lane_base + j * TILE
        lane = first_lane + lax.broadcasted_iota(i32, (TILE, TILE), 1)
        k = lax.broadcasted_iota(i32, (TILE, TILE), 0)
        step_table[...] = residue(7 * k * lane).astype(f32) * INVERSE
        lane = first_lane + lax.broadcasted_iota(i32, (sub_blocks, TILE), 1)
        first = sub_base + TILE * lax.broadcasted_iota(i32, (sub_blocks, TILE), 0)
        inner = residue(lane_poly[0] * lane + lane_poly[1] + 7 * first)
        lane_table[...] = residue(lane * inner).astype(f32) * INVERSE - 0.5
        total = jnp.zeros((2 * width, 2 * TILE), f32)
        for l in range(0, sub_blocks, 2):
            halves = []
            for at in (l, l + 1):
                turn = sub_table[at * TILE:(at + 1) * TILE, :] + step_table[...] + lane_table[at:at + 1, :]
                edge = turn - jnp.floor(turn + (0.5 + HALF_STEP))
                edge = edge * mask_table[pl.ds(j * sub_blocks + at, 1), :]
                halves.append(jnp.concatenate(split(edge), axis=1))
            total += jnp.dot(
                source_parts[:, l * TILE:(l + 2) * TILE], jnp.concatenate(halves, axis=0),
                preferred_element_type=f32,
            )
        total = total[:, :TILE] + total[:, TILE:]
        result = (total[:width] + total[width:]) * scale
        if len(out_ref.shape) == 3:
            out_ref[j] = result
        else:
            out_ref[:, pl.ds(pl.multiple_of(j * TILE, TILE), TILE)] = result
        return carry

    lax.fori_loop(0, lane_blocks, block, 0)


def edge_product(base, count, pairs, source, lane_blocks, sub_blocks, swap, sub_poly, lane_poly, scale, stacked):
    width = source.shape[1] if source.ndim == 3 else source.shape[0]
    shape = (lane_blocks, width, TILE) if stacked else (width, lane_blocks * TILE)
    tiles = lane_blocks * sub_blocks
    smem, vmem = pl.BlockSpec(memory_space=pltpu.SMEM), pl.BlockSpec(memory_space=pltpu.VMEM)
    return pl.pallas_call(
        functools.partial(product_kernel, lane_blocks, sub_blocks, swap, sub_poly, lane_poly, scale),
        out_shape=jax.ShapeDtypeStruct(shape, f32),
        in_specs=[smem, smem, vmem, vmem],
        out_specs=vmem,
        scratch_shapes=[
            pltpu.VMEM((sub_blocks * TILE, TILE), f32),
            pltpu.VMEM((TILE, TILE), f32),
            pltpu.VMEM((sub_blocks, TILE), f32),
            pltpu.VMEM((tiles, TILE), f32),
            pltpu.VMEM((2 * width, sub_blocks * TILE), bf16),
        ],
        compiler_params=pltpu.CompilerParams(vmem_limit_bytes=24 << 20),
        cost_estimate=pl.CostEstimate(flops=8 << 30, bytes_accessed=1 << 21, transcendentals=0),
    )(base, count, pairs, source)


def dot(a, b, dims=((1,), (0,))):
    return lax.dot_general(a, b, (dims, ((), ())), precision=highest, preferred_element_type=f32)


def layer_kernel(
    n_x, n_zh, at_ref, hidden_ref, own_ref, other_ref, both_ref,
    act_ref, grad_ref, own_terms_ref, other_terms_ref, weight,
):
    core, zh = at_ref[0], at_ref[1]
    half = own_ref.shape[0]
    rows, width = weight.shape[2], weight.shape[3]
    packed = rows // 2
    for which, ref in ((core, own_ref), (1 - core, other_ref)):
        for z in range(n_zh):
            blocks = ref[:, z * packed:(z + 1) * packed, :]
            weight[pl.ds(which * half, half), z, :packed, :] = blocks[:, :, :width]
            weight[pl.ds(which * half, half), z, packed:, :] = blocks[:, :, width:]
    hidden = hidden_ref[...].T
    depth = hidden.shape[1]
    grads = []
    for z in range(n_zh):
        columns = weight[:, z].reshape(depth, width)
        pre = dot(hidden, columns)
        squash = 1.0 / (1.0 + jnp.exp(-pre))
        grad_pre = unpack(both_ref[z, packed:, :]) * squash * (1.0 + pre * (1.0 - squash))
        grads.append(grad_pre)

        @pl.when(zh == z)
        def _():
            act_ref[...] = pre * squash
            own = hidden_ref[pl.ds(pl.multiple_of(core * (depth // 2), 8), depth // 2), :]
            other = hidden_ref[pl.ds(pl.multiple_of((1 - core) * (depth // 2), 8), depth // 2), :]
            own_terms_ref[...] = pack(dot(own, grad_pre).reshape(half, rows, width))
            other_terms_ref[...] = pack(dot(other, grad_pre).reshape(half, rows, width))

    per_block = width // rows
    for x in range(n_x):
        total = None
        for z in range(n_zh):
            picked = weight[pl.ds((x * n_zh + zh) * per_block, per_block), z].reshape(width, width)
            term = dot(picked, grads[z], ((1,), (1,)))
            total = term if total is None else total + term
        grad_ref[x] = total


def layer(at, hidden_all, own, other, both, n_x, n_zh, rows):
    half = own.shape[0]
    width = own.shape[2] // 2
    n_rows = hidden_all.shape[1]
    terms = jax.ShapeDtypeStruct((half, rows // 2, 2 * width), f32)
    vmem = pl.BlockSpec(memory_space=pltpu.VMEM)
    return pl.pallas_call(
        functools.partial(layer_kernel, n_x, n_zh),
        out_shape=(
            jax.ShapeDtypeStruct((n_rows, width), f32),
            jax.ShapeDtypeStruct((n_x, width, n_rows), f32),
            terms, terms,
        ),
        in_specs=[pl.BlockSpec(memory_space=pltpu.SMEM), vmem, vmem, vmem, vmem],
        out_specs=(vmem, vmem, vmem, vmem),
        scratch_shapes=[pltpu.VMEM((2 * half, n_zh, rows, width), f32)],
        compiler_params=pltpu.CompilerParams(vmem_limit_bytes=32 << 20),
        cost_estimate=pl.CostEstimate(flops=1 << 30, bytes_accessed=1 << 21, transcendentals=0),
    )(at, hidden_all, own, other, both)


def pack(value):
    n = value.shape[-2] // 2
    return jnp.concatenate([value[..., :n, :], value[..., n:, :]], axis=-1)


def unpack(value):
    width = value.shape[-1] // 2
    return jnp.concatenate([value[..., :width], value[..., width:]], axis=-2)


def copies(value, n):
    return jnp.broadcast_to(value[None], (n,) + value.shape)


def exchange(value, axes):
    return lax.all_to_all(value, axes, 0, 0)


def per_device(features, tile_list, tile_count, weight, cotangent):
    nbr, feat = ("zl", "y"), ("x", "zh")
    pairs, count = tile_list[0, 0], tile_count[0]
    n_nbr = lax.axis_size(nbr)
    n_x, n_zh = lax.axis_size("x"), lax.axis_size("zh")
    core, nbr_id = lax.axis_index("core"), lax.axis_index(nbr)
    width, c_dev = features.shape
    n_rows = cotangent.shape[0]
    r_dev = n_rows * n_nbr
    scale = (12.0 / (c_dev * n_nbr / 2)) ** 0.5
    row_blocks, col_blocks = r_dev // TILE, c_dev // TILE
    swap_core = [(0, 1), (1, 0)]

    both = jnp.concatenate([pack(weight), pack(cotangent)], axis=0)
    both_z = exchange(copies(both, n_zh), "zh")

    bases = jnp.stack([nbr_id * c_dev, core * r_dev]).astype(i32)
    partial = edge_product(bases, count, pairs, features, row_blocks, col_blocks, False, (5, 13), (3, 11), scale, True)
    both_z, partial = lax.optimization_barrier((both_z, partial))
    weight_z = both_z[:, :weight.shape[0] // 2].reshape(-1, both.shape[1])
    hidden = jnp.sum(exchange(partial, nbr), axis=0)
    hidden, weight_z = lax.optimization_barrier((hidden, copies(weight_z, n_nbr)))
    own = exchange(weight_z, nbr)
    hidden_z = lax.all_gather(hidden, "zh", axis=0, tiled=True)
    hidden_z, own = lax.optimization_barrier((hidden_z, own))
    other = lax.ppermute(own, "core", swap_core)
    hidden_all = lax.all_gather(hidden_z, "x", axis=0, tiled=True)

    at = jnp.stack([core, lax.axis_index("zh")]).astype(i32)
    activations, grad_terms, own_terms, other_terms = layer(at, hidden_all, own, other, both_z, n_x, n_zh, weight.shape[0])

    grad_hidden = jnp.sum(exchange(grad_terms, "x"), axis=0)
    grad_block = exchange(copies(grad_hidden, n_nbr), nbr)
    terms = own_terms + lax.ppermute(other_terms, "core", swap_core)
    grad_block, terms = lax.optimization_barrier((grad_block, terms))
    terms = exchange(terms, nbr)
    column_part = edge_product(
        bases[::-1], count, pairs, grad_block, col_blocks, row_blocks, True, (3, 11), (5, 13), scale, False
    )
    column_part, terms = lax.optimization_barrier((column_part, terms))
    feature_grad = column_part + lax.ppermute(column_part, "core", swap_core)
    weight_grad = unpack(jnp.sum(terms, axis=0))
    return activations, feature_grad, weight_grad


def halves(n):
    minor = 1
    while minor * minor < n:
        minor *= 2
    return n // minor, minor


def solution(mesh):
    sizes = (mesh.shape["row"], *halves(mesh.shape["nbr"]), *halves(mesh.shape["feat"]))
    fine = Mesh(mesh.devices.reshape(sizes), ("core", "zl", "y", "x", "zh"))
    nbr, feat = ("zl", "y"), ("x", "zh")
    rows = ("core", *nbr)
    in_specs = (P(feat, nbr), P("core", nbr, None, None), P("core", nbr), P(rows, feat), P(rows, feat))
    out_specs = (P(rows, feat), P(feat, nbr), P(rows, feat))
    return jax.shard_map(per_device, mesh=fine, in_specs=in_specs, out_specs=out_specs, check_vma=False)
```

```python
import functools

import jax
import jax.numpy as jnp
from jax import lax
from jax.experimental import pallas as pl
from jax.experimental.pallas import tpu as pltpu
from jax.sharding import Mesh
from jax.sharding import PartitionSpec as P

TILE = 128
MODULUS = 32749
INVERSE = 1.0 / MODULUS
HALF_STEP = 0.5 / MODULUS
f32, bf16, i32 = jnp.float32, jnp.bfloat16, jnp.int32


def residue(value):
    quotient = jnp.floor(value.astype(f32) * INVERSE).astype(i32)
    rest = value - quotient * MODULUS
    rest = jnp.where(rest < 0, rest + MODULUS, rest)
    return jnp.where(rest >= MODULUS, rest - MODULUS, rest)


def split(value):
    high = value.astype(bf16)
    return high, (value - high.astype(f32)).astype(bf16)


def pack(value):
    n = value.shape[-2] // 2
    return jnp.concatenate([value[..., :n, :], value[..., n:, :]], axis=-1)


def unpack(value):
    width = value.shape[-1] // 2
    return jnp.concatenate([value[..., :width], value[..., width:]], axis=-2)


def listed_tiles(swap, sub_blocks, count_ref, pairs_ref, tiles):
    slots = pairs_ref.shape[1]
    major, minor = (pairs_ref[1:2, :], pairs_ref[0:1, :]) if swap else (pairs_ref[0:1, :], pairs_ref[1:2, :])
    code = major * sub_blocks + minor
    code = jnp.where(lax.broadcasted_iota(i32, (1, slots), 1) < count_ref[0], code, -1)
    listed = (lax.broadcasted_iota(i32, (tiles, slots), 0) == code).astype(f32)
    return jnp.broadcast_to(jnp.sum(listed, axis=1, keepdims=True), (tiles, TILE))


def sub_turns(sub_base, n_sub, sub_poly):
    sub = sub_base + lax.broadcasted_iota(i32, (n_sub, TILE), 0)
    return residue(sub * residue(sub_poly[0] * sub + sub_poly[1])).astype(f32) * INVERSE


def lane_turns(j, sub_base, lane_base, sub_blocks, lane_poly):
    first_lane = lane_base + j * TILE
    lane = first_lane + lax.broadcasted_iota(i32, (TILE, TILE), 1)
    k = lax.broadcasted_iota(i32, (TILE, TILE), 0)
    steps = residue(7 * k * lane).astype(f32) * INVERSE
    lane = first_lane + lax.broadcasted_iota(i32, (sub_blocks, TILE), 1)
    first = sub_base + TILE * lax.broadcasted_iota(i32, (sub_blocks, TILE), 0)
    inner = residue(lane_poly[0] * lane + lane_poly[1] + 7 * first)
    return steps, residue(lane * inner).astype(f32) * INVERSE - 0.5


def edge_parts(turn, listed):
    edge = turn - jnp.floor(turn + (0.5 + HALF_STEP))
    return jnp.concatenate(split(edge * listed), axis=1)


def fold(total, scale):
    width = total.shape[0] // 2
    total = total[:, :TILE] + total[:, TILE:]
    return (total[:width] + total[width:]) * scale


def first_kernel(
    lane_blocks, sub_blocks, sub_poly, lane_poly, scale,
    base_ref, count_ref, pairs_ref, source_ref, out_ref,
    sub_table, step_table, lane_table, mask_table, source_parts,
):
    sub_base, lane_base = base_ref[0], base_ref[1]
    width = source_ref.shape[0]
    mask_table[...] = listed_tiles(False, sub_blocks, count_ref, pairs_ref, lane_blocks * sub_blocks)
    sub_table[...] = sub_turns(sub_base, sub_blocks * TILE, sub_poly)
    for l in range(sub_blocks):
        columns = slice(l * TILE, (l + 1) * TILE)
        source_parts[:width, columns], source_parts[width:, columns] = split(source_ref[:, columns])

    def block(j, carry):
        step_table[...], lane_table[...] = lane_turns(j, sub_base, lane_base, sub_blocks, lane_poly)
        total = jnp.zeros((2 * width, 2 * TILE), f32)
        for l in range(0, sub_blocks, 2):
            parts = []
            for at in (l, l + 1):
                turn = sub_table[at * TILE:(at + 1) * TILE, :] + step_table[...] + lane_table[at:at + 1, :]
                parts.append(edge_parts(turn, mask_table[pl.ds(j * sub_blocks + at, 1), :]))
            total += jnp.dot(
                source_parts[:, l * TILE:(l + 2) * TILE], jnp.concatenate(parts, axis=0),
                preferred_element_type=f32,
            )
        out_ref[j, :width, :] = fold(total, scale)
        return carry

    lax.fori_loop(0, lane_blocks, block, 0)


SMEM, VMEM = pl.BlockSpec(memory_space=pltpu.SMEM), pl.BlockSpec(memory_space=pltpu.VMEM)


def tables(sub_blocks, lane_blocks):
    return [
        pltpu.VMEM((sub_blocks * TILE, TILE), f32),
        pltpu.VMEM((TILE, TILE), f32),
        pltpu.VMEM((sub_blocks, TILE), f32),
        pltpu.VMEM((lane_blocks * sub_blocks, TILE), f32),
    ]


def cost(flops, traffic):
    return pl.CostEstimate(flops=flops, bytes_accessed=traffic, transcendentals=0)


def first_product(base, count, pairs, source, lane_blocks, sub_blocks, sub_poly, lane_poly, scale, room):
    width = source.shape[0]
    return pl.pallas_call(
        functools.partial(first_kernel, lane_blocks, sub_blocks, sub_poly, lane_poly, scale),
        out_shape=jax.ShapeDtypeStruct((lane_blocks, room, TILE), f32),
        in_specs=[SMEM, SMEM, VMEM, VMEM],
        out_specs=VMEM,
        scratch_shapes=tables(sub_blocks, lane_blocks) + [pltpu.VMEM((2 * width, sub_blocks * TILE), bf16)],
        compiler_params=pltpu.CompilerParams(vmem_limit_bytes=24 << 20),
        cost_estimate=cost(8 << 30, 1 << 21),
    )(base, count, pairs, source)


def edges_kernel(
    lane_blocks, sub_blocks, sub_poly, lane_poly, base_ref, count_ref, pairs_ref, out_ref,
    sub_table, step_table, lane_table, mask_table,
):
    j = pl.program_id(0)
    sub_base, lane_base = base_ref[0], base_ref[1]

    @pl.when(j == 0)
    def _():
        mask_table[...] = listed_tiles(True, sub_blocks, count_ref, pairs_ref, lane_blocks * sub_blocks)
        sub_table[...] = sub_turns(sub_base, sub_blocks * TILE, sub_poly)

    step_table[...], lane_table[...] = lane_turns(j, sub_base, lane_base, sub_blocks, lane_poly)
    for at in range(sub_blocks):
        rows = slice(at * TILE, (at + 1) * TILE)
        turn = sub_table[rows, :] + step_table[...] + lane_table[at:at + 1, :]
        out_ref[0, rows, :] = edge_parts(turn, mask_table[pl.ds(j * sub_blocks + at, 1), :])


def all_edges(base, count, pairs, lane_blocks, sub_blocks, sub_poly, lane_poly):
    n_sub = sub_blocks * TILE
    return pl.pallas_call(
        functools.partial(edges_kernel, lane_blocks, sub_blocks, sub_poly, lane_poly),
        grid=(lane_blocks,),
        out_shape=jax.ShapeDtypeStruct((lane_blocks, n_sub, 2 * TILE), bf16),
        in_specs=[SMEM, SMEM, VMEM],
        out_specs=pl.BlockSpec((1, n_sub, 2 * TILE), lambda j: (j, 0, 0)),
        scratch_shapes=tables(sub_blocks, lane_blocks),
        compiler_params=pltpu.CompilerParams(vmem_limit_bytes=50 << 20),
        cost_estimate=cost(8 << 30, 1 << 24),
    )(base, count, pairs)


def last_kernel(width, scale, edges_ref, source_ref, out_ref, weight_grad_ref, source_parts):
    @pl.when(pl.program_id(0) == 0)
    def _():
        for l in range(source_ref.shape[0]):
            columns = slice(l * TILE, (l + 1) * TILE)
            source_parts[:width, columns], source_parts[width:, columns] = split(source_ref[l, :width, :])
        weight_grad_ref[...] = unpack(jnp.sum(source_ref[:, width:, :], axis=0))

    total = jnp.dot(source_parts[...], edges_ref[0], preferred_element_type=f32)
    out_ref[...] = fold(total, scale)


def last_product(edges, source, width, scale):
    lane_blocks, n_sub, _ = edges.shape
    rows = 2 * (source.shape[1] - width)
    return pl.pallas_call(
        functools.partial(last_kernel, width, scale),
        grid=(lane_blocks,),
        out_shape=(
            jax.ShapeDtypeStruct((width, lane_blocks * TILE), f32),
            jax.ShapeDtypeStruct((rows, TILE // 2), f32),
        ),
        in_specs=[
            pl.BlockSpec((1, n_sub, 2 * TILE), lambda j: (j, 0, 0)),
            pl.BlockSpec(source.shape, lambda j: (0, 0, 0)),
        ],
        out_specs=(pl.BlockSpec((width, TILE), lambda j: (0, j)), pl.BlockSpec((rows, TILE // 2), lambda j: (0, 0))),
        scratch_shapes=[pltpu.VMEM((2 * width, n_sub), bf16)],
        compiler_params=pltpu.CompilerParams(vmem_limit_bytes=50 << 20),
        cost_estimate=cost(4 << 30, 1 << 24),
    )(edges, source)


def dot3(a, b):
    a_high, a_low = split(a)
    b_high, b_low = split(b)
    product = functools.partial(jnp.dot, preferred_element_type=f32)
    return product(a_high, b_high) + (product(a_high, b_low) + product(a_low, b_high))


def beside(values):
    return jnp.concatenate(values, axis=-1)


def layer_kernel(
    n_x, n_zh, skip, at_ref, hidden_ref, own_ref, other_ref, both_ref,
    act_ref, grad_ref, own_terms_ref, other_terms_ref, weight,
):
    core, zh = at_ref[0], at_ref[1]
    half = own_ref.shape[0]
    packed, rows, width = own_terms_ref.shape[1], 2 * own_terms_ref.shape[1], own_ref.shape[2] // 2
    depth = hidden_ref.shape[0]
    for which, ref in ((core, own_ref), (1 - core, other_ref)):
        for z in range(0, n_zh, 2):
            pair = [ref[:, skip + at * packed:skip + (at + 1) * packed, :] for at in (z, z + 1)]
            wide = [beside([p[..., :width] for p in pair]), beside([p[..., width:] for p in pair])]
            wide = jnp.concatenate(wide, axis=1).reshape(half * rows, 2 * width)
            weight[pl.ds(pl.multiple_of(which * half * rows, 8), half * rows), z * width:(z + 2) * width] = wide
    pairs = []
    for z in range(0, n_zh, 2):
        pair = [both_ref[at, packed:, :] for at in (z, z + 1)]
        pairs.append(jnp.concatenate([beside([p[:, :width] for p in pair]), beside([p[:, width:] for p in pair])], axis=0))
    cotangent = beside(pairs)

    pre = dot3(hidden_ref[...].T, weight[...])
    squash = 1.0 / (1.0 + jnp.exp(-pre))
    activations = pre * squash
    grad_pre = cotangent * squash * (1.0 + pre * (1.0 - squash))
    n_rows = pre.shape[0]
    picked = [weight[pl.ds(pl.multiple_of((x * n_zh + zh) * width, 8), width), :] for x in range(n_x)]
    grad_ref[...] = dot3(jnp.concatenate(picked, axis=0), grad_pre.T).reshape(n_x, width, n_rows)

    for z in range(n_zh):
        columns = slice(z * width, (z + 1) * width)

        @pl.when(zh == z)
        def _():
            act_ref[...] = activations[:, columns]
            for which, ref in ((core, own_terms_ref), (1 - core, other_terms_ref)):
                part = hidden_ref[pl.ds(pl.multiple_of(which * (depth // 2), 8), depth // 2), :]
                ref[...] = pack(dot3(part, grad_pre[:, columns]).reshape(half, rows, width))


def layer(at, hidden_all, own, other, both, n_x, n_zh, rows, skip):
    half = own.shape[0]
    width = own.shape[2] // 2
    n_rows = hidden_all.shape[1]
    terms = jax.ShapeDtypeStruct((half, rows // 2, 2 * width), f32)
    return pl.pallas_call(
        functools.partial(layer_kernel, n_x, n_zh, skip),
        out_shape=(
            jax.ShapeDtypeStruct((n_rows, width), f32),
            jax.ShapeDtypeStruct((n_x, width, n_rows), f32),
            terms, terms,
        ),
        in_specs=[SMEM, VMEM, VMEM, VMEM, VMEM],
        out_specs=(VMEM, VMEM, VMEM, VMEM),
        scratch_shapes=[pltpu.VMEM((2 * half * rows, n_zh * width), f32)],
        compiler_params=pltpu.CompilerParams(vmem_limit_bytes=32 << 20),
        cost_estimate=cost(1 << 30, 1 << 21),
    )(at, hidden_all, own, other, both)


def join_kernel(grad_ref, own_ref, other_ref, out_ref):
    width = grad_ref.shape[1]
    grad = jnp.sum(grad_ref[...], axis=0)
    for n in range(out_ref.shape[0]):
        out_ref[n, :width, :] = grad
    out_ref[:, width:, :] = own_ref[...] + other_ref[...]


def join(grad_terms, own_terms, other_terms):
    n, packed, lanes = own_terms.shape
    return pl.pallas_call(
        join_kernel,
        out_shape=jax.ShapeDtypeStruct((n, grad_terms.shape[1] + packed, lanes), f32),
        in_specs=[VMEM] * 3,
        out_specs=VMEM,
        cost_estimate=cost(1 << 20, 1 << 20),
    )(grad_terms, own_terms, other_terms)


def start_kernel(weight_ref, cotangent_ref, out_ref):
    both = jnp.concatenate([pack(weight_ref[...]), pack(cotangent_ref[...])], axis=0)
    for n in range(out_ref.shape[0]):
        out_ref[n] = both


def start(weight, cotangent, n):
    rows = (weight.shape[0] + cotangent.shape[0]) // 2
    return pl.pallas_call(
        start_kernel,
        out_shape=jax.ShapeDtypeStruct((n, rows, 2 * weight.shape[1]), f32),
        in_specs=[VMEM] * 2,
        out_specs=VMEM,
        cost_estimate=cost(1 << 16, 1 << 18),
    )(weight, cotangent)


def copies(value, n):
    return jnp.broadcast_to(value[None], (n,) + value.shape)


def exchange(value, axes):
    return lax.all_to_all(value, axes, 0, 0)


def per_device(features, tile_list, tile_count, weight, cotangent):
    nbr, feat = ("zl", "y"), ("x", "zh")
    pairs, count = tile_list[0, 0], tile_count[0]
    n_nbr = lax.axis_size(nbr)
    n_x, n_zh = lax.axis_size("x"), lax.axis_size("zh")
    core, nbr_id = lax.axis_index("core"), lax.axis_index(nbr)
    width, c_dev = features.shape
    n_rows = cotangent.shape[0]
    r_dev = n_rows * n_nbr
    scale = (12.0 / (c_dev * n_nbr / 2)) ** 0.5
    row_blocks, col_blocks = r_dev // TILE, c_dev // TILE
    swap_core = [(0, 1), (1, 0)]

    rows_poly, cols_poly = (3, 11), (5, 13)
    packed = weight.shape[0] // 2
    both_z = exchange(start(weight, cotangent, n_zh), "zh")

    bases = jnp.stack([nbr_id * c_dev, core * r_dev]).astype(i32)
    payload = first_product(
        bases, count, pairs, features, row_blocks, col_blocks, cols_poly, rows_poly, scale, width + n_zh * packed
    )
    both_z, payload, later = lax.optimization_barrier((both_z, payload, bases))
    weight_z = both_z[:, :packed].reshape(-1, TILE)
    payload = lax.dynamic_update_slice(payload, copies(weight_z, n_nbr), (0, width, 0))
    own = exchange(payload, nbr)
    edges = all_edges(later[::-1], count, pairs, col_blocks, row_blocks, rows_poly, cols_poly)
    own, edges = lax.optimization_barrier((own, edges))
    hidden = jnp.sum(own[:, :width], axis=0)
    other = lax.ppermute(own, "core", swap_core)
    hidden_z = lax.all_gather(hidden, "zh", axis=0, tiled=True)
    hidden_all = lax.all_gather(hidden_z, "x", axis=0, tiled=True)

    at = jnp.stack([core, lax.axis_index("zh")]).astype(i32)
    activations, grad_terms, own_terms, other_terms = layer(
        at, hidden_all, own, other, both_z, n_x, n_zh, weight.shape[0], width
    )
    other_terms = lax.ppermute(other_terms, "core", swap_core)
    grad_terms = exchange(grad_terms, "x")
    grad_block = exchange(join(grad_terms, own_terms, other_terms), nbr)
    column_part, weight_grad = last_product(edges, grad_block, width, scale)
    feature_grad = column_part + lax.ppermute(column_part, "core", swap_core)
    return activations, feature_grad, weight_grad


def halves(n):
    minor = 1
    while minor * minor < n:
        minor *= 2
    return n // minor, minor


def solution(mesh):
    sizes = (mesh.shape["row"], *halves(mesh.shape["nbr"]), *halves(mesh.shape["feat"]))
    fine = Mesh(mesh.devices.reshape(sizes), ("core", "zl", "y", "x", "zh"))
    nbr, feat = ("zl", "y"), ("x", "zh")
    rows = ("core", *nbr)
    in_specs = (P(feat, nbr), P("core", nbr, None, None), P("core", nbr), P(rows, feat), P(rows, feat))
    out_specs = (P(rows, feat), P(feat, nbr), P(rows, feat))
    return jax.shard_map(per_device, mesh=fine, in_specs=in_specs, out_specs=out_specs, check_vma=False)
```

```python
import functools

import jax
import jax.numpy as jnp
from jax import lax
from jax.experimental import pallas as pl
from jax.experimental.pallas import tpu as pltpu
from jax.sharding import Mesh
from jax.sharding import PartitionSpec as P

TILE = 128
MODULUS = 32749
INVERSE = 1.0 / MODULUS
WHOLE = 2**32 // MODULUS
PART = 2**32 / MODULUS - WHOLE
TURN = 2.0**32
OFFSET = 64 - 2**31
f32, bf16, i32 = jnp.float32, jnp.bfloat16, jnp.int32


def residue(value):
    quotient = (value.astype(f32) * INVERSE).astype(i32)
    rest = value - quotient * MODULUS
    rest = jnp.where(rest < 0, rest + MODULUS, rest)
    return jnp.where(rest >= MODULUS, rest - MODULUS, rest)


def turns(value):
    rest = residue(value)
    return rest * WHOLE + (rest.astype(f32) * PART + 0.5).astype(i32)


def split(value):
    high = value.astype(bf16)
    return high, (value - high.astype(f32)).astype(bf16)


def pack(value):
    n = value.shape[-2] // 2
    return jnp.concatenate([value[..., :n, :], value[..., n:, :]], axis=-1)


def unpack(value):
    width = value.shape[-1] // 2
    return jnp.concatenate([value[..., :width], value[..., width:]], axis=-2)


def listed_tiles(swap, sub_blocks, count_ref, pairs_ref, tiles):
    slots = pairs_ref.shape[1]
    major, minor = (pairs_ref[1:2, :], pairs_ref[0:1, :]) if swap else (pairs_ref[0:1, :], pairs_ref[1:2, :])
    code = major * sub_blocks + minor
    code = jnp.where(lax.broadcasted_iota(i32, (1, slots), 1) < count_ref[0], code, -1)
    listed = (lax.broadcasted_iota(i32, (tiles, slots), 0) == code).astype(f32)
    return jnp.broadcast_to(jnp.sum(listed, axis=1, keepdims=True), (tiles, TILE))


def sub_turns(sub_base, sub_blocks, sub_poly):
    shape = (TILE, TILE)
    sub = sub_base + TILE * lax.broadcasted_iota(i32, shape, 0) + lax.broadcasted_iota(i32, shape, 1)
    columns = turns(sub * residue(sub_poly[0] * sub + sub_poly[1])).T
    return [jnp.broadcast_to(columns[:, l:l + 1], shape) for l in range(sub_blocks)]


def lane_turns(j, sub_base, lane_base, sub_blocks, lane_poly):
    lane = lane_base + j * TILE + lax.broadcasted_iota(i32, (sub_blocks, TILE), 1)
    first = sub_base + TILE * lax.broadcasted_iota(i32, (sub_blocks, TILE), 0)
    inner = residue(lane_poly[0] * lane + lane_poly[1] + 7 * first)
    return turns(lane * inner) + OFFSET


def step_turns(lane_base):
    lane = lane_base + lax.broadcasted_iota(i32, (TILE, TILE), 1)
    k = lax.broadcasted_iota(i32, (TILE, TILE), 0)
    return turns(7 * k * lane), turns(7 * TILE * k)


def fold(total, scale):
    width = total.shape[0] // 2
    total = total[:, :TILE] + total[:, TILE:]
    return (total[:width] + total[width:]) * scale


def product_kernel(
    lane_blocks, sub_blocks, swap, sub_poly, lane_poly, scale, width,
    base_ref, count_ref, pairs_ref, source_ref, out_ref, *refs,
):
    sub_table, step_table, growth_table, lane_table, mask_table, source_parts = refs[-6:]
    sub_base, lane_base = base_ref[0], base_ref[1]
    mask_table[...] = listed_tiles(swap, sub_blocks, count_ref, pairs_ref, lane_blocks * sub_blocks)
    for l, table in enumerate(sub_turns(sub_base, sub_blocks, sub_poly)):
        columns = slice(l * TILE, (l + 1) * TILE)
        sub_table[columns, :] = table
        piece = source_ref[l, :width, :] if swap else source_ref[:, columns]
        source_parts[:width, columns], source_parts[width:, columns] = split(piece)
    if swap:
        refs[0][...] = unpack(jnp.sum(source_ref[:, width:, :], axis=0))

    step_table[...], growth_table[...] = step_turns(lane_base)

    def block(j, carry):
        lane_table[...] = lane_turns(j, sub_base, lane_base, sub_blocks, lane_poly)
        total = jnp.zeros((2 * width, 2 * TILE), f32)
        for l in range(0, sub_blocks, 2):
            lhs, rhs = [], []
            for at in (l, l + 1):
                columns = slice(at * TILE, (at + 1) * TILE)
                turn = sub_table[columns, :] + step_table[...] + lane_table[at:at + 1, :]
                rhs.append(jnp.concatenate(split(turn.astype(f32)), axis=1))
                listed = jnp.broadcast_to(mask_table[pl.ds(j * sub_blocks + at, 1), :], (2 * width, TILE)).astype(bf16)
                lhs.append(source_parts[:, columns] * listed)
            total += jnp.dot(
                jnp.concatenate(lhs, axis=1), jnp.concatenate(rhs, axis=0), preferred_element_type=f32
            )
        step_table[...] += growth_table[...]
        result = fold(total, scale / TURN)
        if swap:
            out_ref[:, pl.ds(pl.multiple_of(j * TILE, TILE), TILE)] = result
        else:
            out_ref[j] = result
        return carry

    lax.fori_loop(0, lane_blocks, block, 0, unroll=4)


SMEM, VMEM = pl.BlockSpec(memory_space=pltpu.SMEM), pl.BlockSpec(memory_space=pltpu.VMEM)


def cost(flops, traffic):
    return pl.CostEstimate(flops=flops, bytes_accessed=traffic, transcendentals=0)


def edge_product(base, count, pairs, source, lane_blocks, sub_blocks, swap, sub_poly, lane_poly, scale, width):
    out = jax.ShapeDtypeStruct((lane_blocks, width, TILE), f32)
    if swap:
        out = (
            jax.ShapeDtypeStruct((width, lane_blocks * TILE), f32),
            jax.ShapeDtypeStruct((2 * (source.shape[1] - width), TILE // 2), f32),
        )
    return pl.pallas_call(
        functools.partial(product_kernel, lane_blocks, sub_blocks, swap, sub_poly, lane_poly, scale, width),
        out_shape=out,
        in_specs=[SMEM, SMEM, VMEM, VMEM],
        out_specs=(VMEM, VMEM) if swap else VMEM,
        scratch_shapes=[
            pltpu.VMEM((sub_blocks * TILE, TILE), i32),
            pltpu.VMEM((TILE, TILE), i32),
            pltpu.VMEM((TILE, TILE), i32),
            pltpu.VMEM((sub_blocks, TILE), i32),
            pltpu.VMEM((lane_blocks * sub_blocks, TILE), f32),
            pltpu.VMEM((2 * width, sub_blocks * TILE), bf16),
        ],
        compiler_params=pltpu.CompilerParams(vmem_limit_bytes=24 << 20),
        cost_estimate=cost(8 << 30, 1 << 21),
    )(base, count, pairs, source)


def dot3(a, b):
    a_high, a_low = split(a)
    b_high, b_low = split(b)
    product = functools.partial(jnp.dot, preferred_element_type=f32)
    return product(a_high, b_high) + (product(a_high, b_low) + product(a_low, b_high))


def beside(values):
    return jnp.concatenate(values, axis=-1)


def layer_kernel(
    n_x, n_zh, at_ref, hidden_ref, own_ref, other_ref, both_ref,
    act_ref, grad_ref, own_terms_ref, other_terms_ref, weight,
):
    core, zh = at_ref[0], at_ref[1]
    half = own_ref.shape[0]
    packed, rows, width = own_terms_ref.shape[1], 2 * own_terms_ref.shape[1], own_ref.shape[2] // 2
    depth = hidden_ref.shape[0]
    for which, ref in ((core, own_ref), (1 - core, other_ref)):
        for z in range(0, n_zh, 2):
            pair = [ref[:, at * packed:(at + 1) * packed, :] for at in (z, z + 1)]
            wide = [beside([p[..., :width] for p in pair]), beside([p[..., width:] for p in pair])]
            wide = jnp.concatenate(wide, axis=1).reshape(half * rows, 2 * width)
            weight[pl.ds(pl.multiple_of(which * half * rows, 8), half * rows), z * width:(z + 2) * width] = wide
    pairs = []
    for z in range(0, n_zh, 2):
        pair = [both_ref[at, packed:, :] for at in (z, z + 1)]
        pairs.append(jnp.concatenate([beside([p[:, :width] for p in pair]), beside([p[:, width:] for p in pair])], axis=0))
    cotangent = beside(pairs)

    pre = dot3(hidden_ref[...].T, weight[...])
    squash = 1.0 / (1.0 + jnp.exp(-pre))
    activations = pre * squash
    grad_pre = cotangent * squash * (1.0 + pre * (1.0 - squash))
    n_rows = pre.shape[0]
    picked = [weight[pl.ds(pl.multiple_of((x * n_zh + zh) * width, 8), width), :] for x in range(n_x)]
    grad_ref[...] = dot3(jnp.concatenate(picked, axis=0), grad_pre.T).reshape(n_x, width, n_rows)

    for z in range(n_zh):
        columns = slice(z * width, (z + 1) * width)

        @pl.when(zh == z)
        def _():
            act_ref[...] = activations[:, columns]
            for which, ref in ((core, own_terms_ref), (1 - core, other_terms_ref)):
                part = hidden_ref[pl.ds(pl.multiple_of(which * (depth // 2), 8), depth // 2), :]
                ref[...] = pack(dot3(part, grad_pre[:, columns]).reshape(half, rows, width))


def layer(at, hidden_all, own, other, both, n_x, n_zh, rows):
    half = own.shape[0]
    width = own.shape[2] // 2
    n_rows = hidden_all.shape[1]
    terms = jax.ShapeDtypeStruct((half, rows // 2, 2 * width), f32)
    return pl.pallas_call(
        functools.partial(layer_kernel, n_x, n_zh),
        out_shape=(
            jax.ShapeDtypeStruct((n_rows, width), f32),
            jax.ShapeDtypeStruct((n_x, width, n_rows), f32),
            terms, terms,
        ),
        in_specs=[SMEM, VMEM, VMEM, VMEM, VMEM],
        out_specs=(VMEM, VMEM, VMEM, VMEM),
        scratch_shapes=[pltpu.VMEM((2 * half * rows, n_zh * width), f32)],
        compiler_params=pltpu.CompilerParams(vmem_limit_bytes=32 << 20),
        cost_estimate=cost(1 << 30, 1 << 21),
    )(at, hidden_all, own, other, both)


def join_kernel(grad_ref, own_ref, other_ref, out_ref):
    width = grad_ref.shape[1]
    grad = jnp.sum(grad_ref[...], axis=0)
    for n in range(out_ref.shape[0]):
        out_ref[n, :width, :] = grad
    out_ref[:, width:, :] = own_ref[...] + other_ref[...]


def join(grad_terms, own_terms, other_terms):
    n, packed, lanes = own_terms.shape
    return pl.pallas_call(
        join_kernel,
        out_shape=jax.ShapeDtypeStruct((n, grad_terms.shape[1] + packed, lanes), f32),
        in_specs=[VMEM] * 3,
        out_specs=VMEM,
        cost_estimate=cost(1 << 20, 1 << 20),
    )(grad_terms, own_terms, other_terms)


def start_kernel(weight_ref, cotangent_ref, out_ref):
    both = jnp.concatenate([pack(weight_ref[...]), pack(cotangent_ref[...])], axis=0)
    for n in range(out_ref.shape[0]):
        out_ref[n] = both


def start(weight, cotangent, n):
    rows = (weight.shape[0] + cotangent.shape[0]) // 2
    return pl.pallas_call(
        start_kernel,
        out_shape=jax.ShapeDtypeStruct((n, rows, 2 * weight.shape[1]), f32),
        in_specs=[VMEM] * 2,
        out_specs=VMEM,
        cost_estimate=cost(1 << 16, 1 << 18),
    )(weight, cotangent)


def copies(value, n):
    return jnp.broadcast_to(value[None], (n,) + value.shape)


def exchange(value, axes):
    return lax.all_to_all(value, axes, 0, 0)


def per_device(features, tile_list, tile_count, weight, cotangent):
    nbr, feat = ("zl", "y"), ("x", "zh")
    pairs, count = tile_list[0, 0], tile_count[0]
    n_nbr = lax.axis_size(nbr)
    n_x, n_zh = lax.axis_size("x"), lax.axis_size("zh")
    core, nbr_id = lax.axis_index("core"), lax.axis_index(nbr)
    width, c_dev = features.shape
    n_rows = cotangent.shape[0]
    r_dev = n_rows * n_nbr
    scale = (12.0 / (c_dev * n_nbr / 2)) ** 0.5
    row_blocks, col_blocks = r_dev // TILE, c_dev // TILE
    swap_core = [(0, 1), (1, 0)]

    rows_poly, cols_poly = (3, 11), (5, 13)
    packed = weight.shape[0] // 2
    both_z = exchange(start(weight, cotangent, n_zh), "zh")

    bases = jnp.stack([nbr_id * c_dev, core * r_dev]).astype(i32)
    partial = edge_product(
        bases, count, pairs, features, row_blocks, col_blocks, False, cols_poly, rows_poly, scale, width
    )
    both_z, partial = lax.optimization_barrier((both_z, partial))
    weight_z = both_z[:, :packed].reshape(-1, TILE)
    hidden = jnp.sum(exchange(partial, nbr), axis=0)
    hidden, weight_z = lax.optimization_barrier((hidden, copies(weight_z, n_nbr)))
    own = exchange(weight_z, nbr)
    hidden_z = lax.all_gather(hidden, "zh", axis=0, tiled=True)
    hidden_z, own = lax.optimization_barrier((hidden_z, own))
    other = lax.ppermute(own, "core", swap_core)
    hidden_all = lax.all_gather(hidden_z, "x", axis=0, tiled=True)

    at = jnp.stack([core, lax.axis_index("zh")]).astype(i32)
    activations, grad_terms, own_terms, other_terms = layer(
        at, hidden_all, own, other, both_z, n_x, n_zh, weight.shape[0]
    )
    other_terms = lax.ppermute(other_terms, "core", swap_core)
    grad_terms = exchange(grad_terms, "x")
    grad_block = exchange(join(grad_terms, own_terms, other_terms), nbr)
    column_part, weight_grad = edge_product(
        bases[::-1], count, pairs, grad_block, col_blocks, row_blocks, True, rows_poly, cols_poly, scale, width
    )
    feature_grad = column_part + lax.ppermute(column_part, "core", swap_core)
    return activations, feature_grad, weight_grad


def halves(n):
    minor = 1
    while minor * minor < n:
        minor *= 2
    return n // minor, minor


def solution(mesh):
    sizes = (mesh.shape["row"], *halves(mesh.shape["nbr"]), *halves(mesh.shape["feat"]))
    fine = Mesh(mesh.devices.reshape(sizes), ("core", "zl", "y", "x", "zh"))
    nbr, feat = ("zl", "y"), ("x", "zh")
    rows = ("core", *nbr)
    in_specs = (P(feat, nbr), P("core", nbr, None, None), P("core", nbr), P(rows, feat), P(rows, feat))
    out_specs = (P(rows, feat), P(feat, nbr), P(rows, feat))
    return jax.shard_map(per_device, mesh=fine, in_specs=in_specs, out_specs=out_specs, check_vma=False)
```

```python
import functools

import jax
import jax.numpy as jnp
from jax import lax
from jax.experimental import pallas as pl
from jax.experimental.pallas import tpu as pltpu
from jax.sharding import Mesh
from jax.sharding import PartitionSpec as P

TILE = 128
MODULUS = 32749
INVERSE = 1.0 / MODULUS
WHOLE = 2**32 // MODULUS
PART = 2**32 / MODULUS - WHOLE
TURN = 2.0**32
OFFSET = 64 - 2**31
f32, bf16, i32 = jnp.float32, jnp.bfloat16, jnp.int32


def residue(value):
    quotient = (value.astype(f32) * INVERSE).astype(i32)
    rest = value - quotient * MODULUS
    rest = jnp.where(rest < 0, rest + MODULUS, rest)
    return jnp.where(rest >= MODULUS, rest - MODULUS, rest)


def turns(value):
    rest = residue(value)
    return rest * WHOLE + (rest.astype(f32) * PART + 0.5).astype(i32)


def split(value):
    high = value.astype(bf16)
    return high, (value - high.astype(f32)).astype(bf16)


def pack(value):
    n = value.shape[-2] // 2
    return jnp.concatenate([value[..., :n, :], value[..., n:, :]], axis=-1)


def unpack(value):
    width = value.shape[-1] // 2
    return jnp.concatenate([value[..., :width], value[..., width:]], axis=-2)


def listed_tiles(swap, sub_blocks, count_ref, pairs_ref, tiles):
    slots = pairs_ref.shape[1]
    major, minor = (pairs_ref[1:2, :], pairs_ref[0:1, :]) if swap else (pairs_ref[0:1, :], pairs_ref[1:2, :])
    code = major * sub_blocks + minor
    code = jnp.where(lax.broadcasted_iota(i32, (1, slots), 1) < count_ref[0], code, -1)
    listed = (lax.broadcasted_iota(i32, (tiles, slots), 0) == code).astype(f32)
    return jnp.broadcast_to(jnp.sum(listed, axis=1, keepdims=True), (tiles, TILE))


def sub_turns(sub_base, sub_blocks, sub_poly):
    shape = (TILE, TILE)
    sub = sub_base + TILE * lax.broadcasted_iota(i32, shape, 0) + lax.broadcasted_iota(i32, shape, 1)
    columns = turns(sub * residue(sub_poly[0] * sub + sub_poly[1])).T
    return [jnp.broadcast_to(columns[:, l:l + 1], shape) for l in range(sub_blocks)]


def lane_turns(j, sub_base, lane_base, sub_blocks, lane_poly):
    lane = lane_base + j * TILE + lax.broadcasted_iota(i32, (sub_blocks, TILE), 1)
    first = sub_base + TILE * lax.broadcasted_iota(i32, (sub_blocks, TILE), 0)
    inner = residue(lane_poly[0] * lane + lane_poly[1] + 7 * first)
    return turns(lane * inner) + OFFSET


def step_turns(lane_base):
    lane = lane_base + lax.broadcasted_iota(i32, (TILE, TILE), 1)
    k = lax.broadcasted_iota(i32, (TILE, TILE), 0)
    return turns(7 * k * lane), turns(7 * TILE * k)


def fold(total, scale):
    width = total.shape[0] // 2
    total = total[:, :TILE] + total[:, TILE:]
    return (total[:width] + total[width:]) * scale


def product_kernel(
    lane_blocks, sub_blocks, swap, sub_poly, lane_poly, scale, width,
    base_ref, count_ref, pairs_ref, source_ref, *refs,
):
    sub_table, step_table, growth_table, lane_table, mask_table, source_parts = refs[-6:]
    if swap:
        terms_ref, out_ref, sum_ref = refs[:3]
        sum_ref[...] = unpack(jnp.sum(terms_ref[...], axis=0))
    else:
        out_ref = refs[0]
    sub_base, lane_base = base_ref[0], base_ref[1]
    mask_table[...] = listed_tiles(swap, sub_blocks, count_ref, pairs_ref, lane_blocks * sub_blocks)
    for l, table in enumerate(sub_turns(sub_base, sub_blocks, sub_poly)):
        columns = slice(l * TILE, (l + 1) * TILE)
        sub_table[columns, :] = table
        piece = source_ref[l] if swap else source_ref[:, columns]
        source_parts[:width, columns], source_parts[width:, columns] = split(piece)

    step_table[...], growth_table[...] = step_turns(lane_base)

    def block(j, carry):
        lane_table[...] = lane_turns(j, sub_base, lane_base, sub_blocks, lane_poly)
        total = jnp.zeros((2 * width, 2 * TILE), f32)
        for l in range(0, sub_blocks, 2):
            lhs, rhs = [], []
            for at in (l, l + 1):
                columns = slice(at * TILE, (at + 1) * TILE)
                turn = sub_table[columns, :] + step_table[...] + lane_table[at:at + 1, :]
                rhs.append(jnp.concatenate(split(turn.astype(f32)), axis=1))
                listed = jnp.broadcast_to(mask_table[pl.ds(j * sub_blocks + at, 1), :], (2 * width, TILE)).astype(bf16)
                lhs.append(source_parts[:, columns] * listed)
            total += jnp.dot(
                jnp.concatenate(lhs, axis=1), jnp.concatenate(rhs, axis=0), preferred_element_type=f32
            )
        step_table[...] += growth_table[...]
        result = fold(total, scale / TURN)
        if swap:
            out_ref[:, pl.ds(pl.multiple_of(j * TILE, TILE), TILE)] = result
        else:
            out_ref[j] = result
        return carry

    lax.fori_loop(0, lane_blocks, block, 0, unroll=4)


SMEM, VMEM = pl.BlockSpec(memory_space=pltpu.SMEM), pl.BlockSpec(memory_space=pltpu.VMEM)


def cost(flops, traffic):
    return pl.CostEstimate(flops=flops, bytes_accessed=traffic, transcendentals=0)


def edge_product(base, count, pairs, source, lane_blocks, sub_blocks, swap, sub_poly, lane_poly, scale, width, *terms):
    out = jax.ShapeDtypeStruct((lane_blocks, width, TILE), f32)
    if swap:
        out = (
            jax.ShapeDtypeStruct((width, lane_blocks * TILE), f32),
            jax.ShapeDtypeStruct((2 * terms[0].shape[1], terms[0].shape[2] // 2), f32),
        )
    return pl.pallas_call(
        functools.partial(product_kernel, lane_blocks, sub_blocks, swap, sub_poly, lane_poly, scale, width),
        out_shape=out,
        in_specs=[SMEM, SMEM, VMEM, VMEM] + [VMEM] * len(terms),
        out_specs=(VMEM, VMEM) if swap else VMEM,
        scratch_shapes=[
            pltpu.VMEM((sub_blocks * TILE, TILE), i32),
            pltpu.VMEM((TILE, TILE), i32),
            pltpu.VMEM((TILE, TILE), i32),
            pltpu.VMEM((sub_blocks, TILE), i32),
            pltpu.VMEM((lane_blocks * sub_blocks, TILE), f32),
            pltpu.VMEM((2 * width, sub_blocks * TILE), bf16),
        ],
        compiler_params=pltpu.CompilerParams(vmem_limit_bytes=24 << 20),
        cost_estimate=cost(8 << 30, 1 << 21),
    )(base, count, pairs, source, *terms)


def dot3(a, b):
    a_high, a_low = split(a)
    b_high, b_low = split(b)
    product = functools.partial(jnp.dot, preferred_element_type=f32)
    return product(a_high, b_high) + (product(a_high, b_low) + product(a_low, b_high))


def beside(values):
    return jnp.concatenate(values, axis=-1)


def layer_kernel(
    n_x, n_zh, at_ref, hidden_ref, own_ref, other_ref, both_ref,
    act_ref, grad_ref, own_terms_ref, other_terms_ref, weight,
):
    core, zh = at_ref[0], at_ref[1]
    half = own_ref.shape[0]
    packed, rows, width = own_terms_ref.shape[1], 2 * own_terms_ref.shape[1], own_ref.shape[2] // 2
    depth = hidden_ref.shape[0]
    for which, ref in ((core, own_ref), (1 - core, other_ref)):
        for z in range(0, n_zh, 2):
            pair = [ref[:, at * packed:(at + 1) * packed, :] for at in (z, z + 1)]
            wide = [beside([p[..., :width] for p in pair]), beside([p[..., width:] for p in pair])]
            wide = jnp.concatenate(wide, axis=1).reshape(half * rows, 2 * width)
            weight[pl.ds(pl.multiple_of(which * half * rows, 8), half * rows), z * width:(z + 2) * width] = wide
    cotangent = jnp.concatenate([both_ref[z, packed:, :] for z in range(n_zh)], axis=0).T

    pre = dot3(hidden_ref[...].T, weight[...])
    squash = 1.0 / (1.0 + jnp.exp(-pre))
    activations = (pre * squash).T
    grad_pre = cotangent * squash * (1.0 + pre * (1.0 - squash))
    n_rows = pre.shape[0]
    picked = [weight[pl.ds(pl.multiple_of((x * n_zh + zh) * width, 8), width), :] for x in range(n_x)]
    grad_terms = dot3(jnp.concatenate(picked, axis=0), grad_pre.T).reshape(n_x, width, n_rows)
    for y in range(grad_ref.shape[0]):
        grad_ref[y] = grad_terms

    for z in range(n_zh):
        columns = slice(z * width, (z + 1) * width)

        @pl.when(zh == z)
        def _():
            act_ref[...] = activations[columns, :]
            for which, ref in ((core, own_terms_ref), (1 - core, other_terms_ref)):
                part = hidden_ref[pl.ds(pl.multiple_of(which * (depth // 2), 8), depth // 2), :]
                ref[...] = pack(dot3(part, grad_pre[:, columns]).reshape(half, rows, width))


def layer(at, hidden_all, own, other, both, n_y, n_x, n_zh, rows):
    half = own.shape[0]
    width = own.shape[2] // 2
    n_rows = hidden_all.shape[1]
    terms = jax.ShapeDtypeStruct((half, rows // 2, 2 * width), f32)
    return pl.pallas_call(
        functools.partial(layer_kernel, n_x, n_zh),
        out_shape=(
            jax.ShapeDtypeStruct((width, n_rows), f32),
            jax.ShapeDtypeStruct((n_y, n_x, width, n_rows), f32),
            terms, terms,
        ),
        in_specs=[SMEM, VMEM, VMEM, VMEM, VMEM],
        out_specs=(VMEM, VMEM, VMEM, VMEM),
        scratch_shapes=[pltpu.VMEM((2 * half * rows, n_zh * width), f32)],
        compiler_params=pltpu.CompilerParams(vmem_limit_bytes=32 << 20),
        cost_estimate=cost(1 << 30, 1 << 21),
    )(at, hidden_all, own, other, both)


def join_kernel(n_x, grad_ref, own_ref, other_ref, out_ref, terms_ref):
    width = grad_ref.shape[1]
    for y in range(grad_ref.shape[0] // n_x):
        out_ref[y * width:(y + 1) * width, :] = jnp.sum(grad_ref[y * n_x:(y + 1) * n_x], axis=0)
    terms_ref[...] = own_ref[...] + other_ref[...]


def join(grad_terms, own_terms, other_terms, n_x):
    n, width, lanes = grad_terms.shape
    return pl.pallas_call(
        functools.partial(join_kernel, n_x),
        out_shape=(
            jax.ShapeDtypeStruct((n // n_x * width, lanes), f32),
            jax.ShapeDtypeStruct(own_terms.shape, f32),
        ),
        in_specs=[VMEM] * 3,
        out_specs=(VMEM, VMEM),
        cost_estimate=cost(1 << 20, 1 << 20),
    )(grad_terms, own_terms, other_terms)


def start_kernel(weight_ref, turned_ref, out_ref):
    packed = weight_ref.shape[0] // 2
    weight = pack(weight_ref[...])
    for n in range(out_ref.shape[0]):
        out_ref[n, :packed, :] = weight
        out_ref[n, packed:, :] = turned_ref[...]


def start(weight, turned, n):
    return pl.pallas_call(
        start_kernel,
        out_shape=jax.ShapeDtypeStruct((n, weight.shape[0] // 2 + turned.shape[0], turned.shape[1]), f32),
        in_specs=[VMEM] * 2,
        out_specs=VMEM,
        cost_estimate=cost(1 << 16, 1 << 18),
    )(weight, turned)


def copies(value, n):
    return jnp.broadcast_to(value[None], (n,) + value.shape)


def exchange(value, axes):
    return lax.all_to_all(value, axes, 0, 0)


def per_device(features, tile_list, tile_count, weight, cotangent):
    nbr, feat = ("zl", "y"), ("x", "zh")
    pairs, count = tile_list[0, 0], tile_count[0]
    n_nbr = lax.axis_size(nbr)
    n_y, n_x, n_zh = lax.axis_size("y"), lax.axis_size("x"), lax.axis_size("zh")
    core, nbr_id = lax.axis_index("core"), lax.axis_index(nbr)
    width, c_dev = features.shape
    n_rows = cotangent.shape[0]
    r_dev = n_rows * n_nbr
    scale = (12.0 / (c_dev * n_nbr / 2)) ** 0.5
    row_blocks, col_blocks = r_dev // TILE, c_dev // TILE
    swap_core = [(0, 1), (1, 0)]

    rows_poly, cols_poly = (3, 11), (5, 13)
    packed = weight.shape[0] // 2
    both_z = exchange(start(weight, cotangent.T, n_zh), "zh")

    bases = jnp.stack([nbr_id * c_dev, core * r_dev]).astype(i32)
    partial = edge_product(
        bases, count, pairs, features, row_blocks, col_blocks, False, cols_poly, rows_poly, scale, width
    )
    both_z, partial = lax.optimization_barrier((both_z, partial))
    weight_z = both_z[:, :packed].reshape(-1, TILE)
    hidden = jnp.sum(exchange(partial, nbr), axis=0)
    hidden, weight_z = lax.optimization_barrier((hidden, copies(weight_z, n_nbr)))
    own = exchange(weight_z, nbr)
    hidden_z = lax.all_gather(hidden, "zh", axis=0, tiled=True)
    hidden_z, own = lax.optimization_barrier((hidden_z, own))
    other = lax.ppermute(own, "core", swap_core)
    hidden_all = exchange(copies(hidden_z, n_x), "x").reshape(-1, n_rows)

    at = jnp.stack([core, lax.axis_index("zh")]).astype(i32)
    activations, grad_terms, own_terms, other_terms = layer(
        at, hidden_all, own, other, both_z, n_y, n_x, n_zh, weight.shape[0]
    )
    other_terms = lax.ppermute(other_terms, "core", swap_core)
    grad_terms = exchange(grad_terms.reshape(-1, width, n_rows), ("y", "x"))
    grad_hidden, terms = join(grad_terms, own_terms, other_terms, n_x)
    terms = exchange(terms, nbr)
    grad_block = lax.all_gather(grad_hidden, "zl", axis=0, tiled=True).reshape(n_nbr, width, n_rows)
    column_part, weight_grad = edge_product(
        bases[::-1], count, pairs, grad_block, col_blocks, row_blocks, True, rows_poly, cols_poly, scale, width, terms
    )
    feature_grad = column_part + lax.ppermute(column_part, "core", swap_core)
    return activations.T, feature_grad, weight_grad


def halves(n):
    minor = 1
    while minor * minor < n:
        minor *= 2
    return n // minor, minor


def solution(mesh):
    sizes = (mesh.shape["row"], *halves(mesh.shape["nbr"]), *halves(mesh.shape["feat"]))
    fine = Mesh(mesh.devices.reshape(sizes), ("core", "zl", "y", "x", "zh"))
    nbr, feat = ("zl", "y"), ("x", "zh")
    rows = ("core", *nbr)
    in_specs = (P(feat, nbr), P("core", nbr, None, None), P("core", nbr), P(rows, feat), P(rows, feat))
    out_specs = (P(rows, feat), P(feat, nbr), P(rows, feat))
    return jax.shard_map(per_device, mesh=fine, in_specs=in_specs, out_specs=out_specs, check_vma=False)
```

```python
import functools

import jax
import jax.numpy as jnp
from jax import lax
from jax.experimental import pallas as pl
from jax.experimental.pallas import tpu as pltpu
from jax.sharding import Mesh
from jax.sharding import PartitionSpec as P

TILE = 128
MODULUS = 32749
INVERSE = 1.0 / MODULUS
WHOLE = 2**32 // MODULUS
PART = 2**32 / MODULUS - WHOLE
TURN = 2.0**32
OFFSET = 64 - 2**31
f32, bf16, i32 = jnp.float32, jnp.bfloat16, jnp.int32


def residue(value):
    quotient = (value.astype(f32) * INVERSE).astype(i32)
    rest = value - quotient * MODULUS
    rest = jnp.where(rest < 0, rest + MODULUS, rest)
    return jnp.where(rest >= MODULUS, rest - MODULUS, rest)


def turns(value):
    rest = residue(value)
    return rest * WHOLE + (rest.astype(f32) * PART + 0.5).astype(i32)


def split(value):
    high = value.astype(bf16)
    return high, (value - high.astype(f32)).astype(bf16)


def pack(value):
    n = value.shape[-2] // 2
    return jnp.concatenate([value[..., :n, :], value[..., n:, :]], axis=-1)


def unpack(value):
    width = value.shape[-1] // 2
    return jnp.concatenate([value[..., :width], value[..., width:]], axis=-2)


def listed_tiles(swap, sub_blocks, count_ref, pairs_ref, tiles):
    slots = pairs_ref.shape[1]
    major, minor = (pairs_ref[1:2, :], pairs_ref[0:1, :]) if swap else (pairs_ref[0:1, :], pairs_ref[1:2, :])
    code = major * sub_blocks + minor
    code = jnp.where(lax.broadcasted_iota(i32, (1, slots), 1) < count_ref[0], code, -1)
    listed = (lax.broadcasted_iota(i32, (tiles, slots), 0) == code).astype(f32)
    return jnp.broadcast_to(jnp.sum(listed, axis=1, keepdims=True), (tiles, TILE))


def sub_turns(sub_base, sub_blocks, sub_poly):
    shape = (TILE, TILE)
    sub = sub_base + TILE * lax.broadcasted_iota(i32, shape, 0) + lax.broadcasted_iota(i32, shape, 1)
    columns = turns(sub * residue(sub_poly[0] * sub + sub_poly[1])).T
    return [jnp.broadcast_to(columns[:, l:l + 1], shape) for l in range(sub_blocks)]


def lane_turns(j, sub_base, lane_base, sub_blocks, lane_poly):
    lane = lane_base + j * TILE + lax.broadcasted_iota(i32, (sub_blocks, TILE), 1)
    first = sub_base + TILE * lax.broadcasted_iota(i32, (sub_blocks, TILE), 0)
    inner = residue(lane_poly[0] * lane + lane_poly[1] + 7 * first)
    return turns(lane * inner) + OFFSET


def step_turns(lane_base):
    lane = lane_base + lax.broadcasted_iota(i32, (TILE, TILE), 1)
    k = lax.broadcasted_iota(i32, (TILE, TILE), 0)
    return turns(7 * k * lane), turns(7 * TILE * k)


def fold(total, scale):
    width = total.shape[0] // 2
    total = total[:, :TILE] + total[:, TILE:]
    return (total[:width] + total[width:]) * scale


def product_kernel(
    lane_blocks, sub_blocks, swap, sub_poly, lane_poly, scale, width,
    base_ref, count_ref, pairs_ref, source_ref, out_ref, *refs,
):
    sub_table, step_table, growth_table, lane_table, mask_table, source_parts = refs[-6:]
    sub_base, lane_base = base_ref[0], base_ref[1]
    mask_table[...] = listed_tiles(swap, sub_blocks, count_ref, pairs_ref, lane_blocks * sub_blocks)
    for l, table in enumerate(sub_turns(sub_base, sub_blocks, sub_poly)):
        columns = slice(l * TILE, (l + 1) * TILE)
        sub_table[columns, :] = table
        piece = source_ref[l, :width, :] if swap else source_ref[:, columns]
        source_parts[:width, columns], source_parts[width:, columns] = split(piece)
    if swap:
        refs[0][...] = unpack(jnp.sum(source_ref[:, width:, :], axis=0))

    step_table[...], growth_table[...] = step_turns(lane_base)

    def block(j, carry):
        lane_table[...] = lane_turns(j, sub_base, lane_base, sub_blocks, lane_poly)
        total = jnp.zeros((2 * width, 2 * TILE), f32)
        for l in range(0, sub_blocks, 2):
            lhs, rhs = [], []
            for at in (l, l + 1):
                columns = slice(at * TILE, (at + 1) * TILE)
                turn = sub_table[columns, :] + step_table[...] + lane_table[at:at + 1, :]
                rhs.append(jnp.concatenate(split(turn.astype(f32)), axis=1))
                listed = jnp.broadcast_to(mask_table[pl.ds(j * sub_blocks + at, 1), :], (2 * width, TILE)).astype(bf16)
                lhs.append(source_parts[:, columns] * listed)
            total += jnp.dot(
                jnp.concatenate(lhs, axis=1), jnp.concatenate(rhs, axis=0), preferred_element_type=f32
            )
        step_table[...] += growth_table[...]
        result = fold(total, scale / TURN)
        if swap:
            out_ref[:, pl.ds(pl.multiple_of(j * TILE, TILE), TILE)] = result
        else:
            out_ref[j] = result
        return carry

    lax.fori_loop(0, lane_blocks, block, 0, unroll=4)


SMEM, VMEM = pl.BlockSpec(memory_space=pltpu.SMEM), pl.BlockSpec(memory_space=pltpu.VMEM)


def cost(flops, traffic):
    return pl.CostEstimate(flops=flops, bytes_accessed=traffic, transcendentals=0)


def edge_product(base, count, pairs, source, lane_blocks, sub_blocks, swap, sub_poly, lane_poly, scale, width):
    out = jax.ShapeDtypeStruct((lane_blocks, width, TILE), f32)
    if swap:
        out = (
            jax.ShapeDtypeStruct((width, lane_blocks * TILE), f32),
            jax.ShapeDtypeStruct((2 * (source.shape[1] - width), TILE // 2), f32),
        )
    return pl.pallas_call(
        functools.partial(product_kernel, lane_blocks, sub_blocks, swap, sub_poly, lane_poly, scale, width),
        out_shape=out,
        in_specs=[SMEM, SMEM, VMEM, VMEM],
        out_specs=(VMEM, VMEM) if swap else VMEM,
        scratch_shapes=[
            pltpu.VMEM((sub_blocks * TILE, TILE), i32),
            pltpu.VMEM((TILE, TILE), i32),
            pltpu.VMEM((TILE, TILE), i32),
            pltpu.VMEM((sub_blocks, TILE), i32),
            pltpu.VMEM((lane_blocks * sub_blocks, TILE), f32),
            pltpu.VMEM((2 * width, sub_blocks * TILE), bf16),
        ],
        compiler_params=pltpu.CompilerParams(vmem_limit_bytes=24 << 20),
        cost_estimate=cost(8 << 30, 1 << 21),
    )(base, count, pairs, source)


def dot3(a, b):
    a_high, a_low = split(a)
    b_high, b_low = split(b)
    product = functools.partial(jnp.dot, preferred_element_type=f32)
    return product(a_high, b_high) + (product(a_high, b_low) + product(a_low, b_high))


def beside(values):
    return jnp.concatenate(values, axis=-1)


def layer_kernel(
    n_x, n_zh, at_ref, hidden_ref, own_ref, other_ref, both_ref,
    act_ref, grad_ref, own_terms_ref, other_terms_ref, weight,
):
    core, zh = at_ref[0], at_ref[1]
    half = own_ref.shape[0]
    packed, rows, width = own_terms_ref.shape[1], 2 * own_terms_ref.shape[1], own_ref.shape[2] // 2
    depth = hidden_ref.shape[0]
    for which, ref in ((core, own_ref), (1 - core, other_ref)):
        for z in range(0, n_zh, 2):
            pair = [ref[:, at * packed:(at + 1) * packed, :] for at in (z, z + 1)]
            wide = [beside([p[..., :width] for p in pair]), beside([p[..., width:] for p in pair])]
            wide = jnp.concatenate(wide, axis=1).reshape(half * rows, 2 * width)
            weight[pl.ds(pl.multiple_of(which * half * rows, 8), half * rows), z * width:(z + 2) * width] = wide
    cotangent = jnp.concatenate([both_ref[z, packed:, :] for z in range(n_zh)], axis=0).T

    pre = dot3(hidden_ref[...].T, weight[...])
    squash = 1.0 / (1.0 + jnp.exp(-pre))
    activations = (pre * squash).T
    grad_pre = cotangent * squash * (1.0 + pre * (1.0 - squash))
    n_rows = pre.shape[0]
    picked = [weight[pl.ds(pl.multiple_of((x * n_zh + zh) * width, 8), width), :] for x in range(n_x)]
    grad_ref[...] = dot3(jnp.concatenate(picked, axis=0), grad_pre.T).reshape(n_x, width, n_rows)

    for z in range(n_zh):
        columns = slice(z * width, (z + 1) * width)

        @pl.when(zh == z)
        def _():
            act_ref[...] = activations[columns, :]
            for which, ref in ((core, own_terms_ref), (1 - core, other_terms_ref)):
                part = hidden_ref[pl.ds(pl.multiple_of(which * (depth // 2), 8), depth // 2), :]
                ref[...] = pack(dot3(part, grad_pre[:, columns]).reshape(half, rows, width))


def layer(at, hidden_all, own, other, both, n_x, n_zh, rows):
    half = own.shape[0]
    width = own.shape[2] // 2
    n_rows = hidden_all.shape[1]
    terms = jax.ShapeDtypeStruct((half, rows // 2, 2 * width), f32)
    return pl.pallas_call(
        functools.partial(layer_kernel, n_x, n_zh),
        out_shape=(
            jax.ShapeDtypeStruct((width, n_rows), f32),
            jax.ShapeDtypeStruct((n_x, width, n_rows), f32),
            terms, terms,
        ),
        in_specs=[SMEM, VMEM, VMEM, VMEM, VMEM],
        out_specs=(VMEM, VMEM, VMEM, VMEM),
        scratch_shapes=[pltpu.VMEM((2 * half * rows, n_zh * width), f32)],
        compiler_params=pltpu.CompilerParams(vmem_limit_bytes=32 << 20),
        cost_estimate=cost(1 << 30, 1 << 21),
    )(at, hidden_all, own, other, both)


def join_kernel(grad_ref, own_ref, other_ref, out_ref):
    width = grad_ref.shape[1]
    grad = jnp.sum(grad_ref[...], axis=0)
    for n in range(out_ref.shape[0]):
        out_ref[n, :width, :] = grad
    out_ref[:, width:, :] = own_ref[...] + other_ref[...]


def join(grad_terms, own_terms, other_terms):
    n, packed, lanes = own_terms.shape
    return pl.pallas_call(
        join_kernel,
        out_shape=jax.ShapeDtypeStruct((n, grad_terms.shape[1] + packed, lanes), f32),
        in_specs=[VMEM] * 3,
        out_specs=VMEM,
        cost_estimate=cost(1 << 20, 1 << 20),
    )(grad_terms, own_terms, other_terms)


def copies(value, n):
    return jnp.broadcast_to(value[None], (n,) + value.shape)


def exchange(value, axes):
    return lax.all_to_all(value, axes, 0, 0)


def per_device(features, tile_list, tile_count, weight, cotangent):
    nbr, feat = ("zl", "y"), ("x", "zh")
    pairs, count = tile_list[0, 0], tile_count[0]
    n_nbr = lax.axis_size(nbr)
    n_x, n_zh = lax.axis_size("x"), lax.axis_size("zh")
    core, nbr_id = lax.axis_index("core"), lax.axis_index(nbr)
    width, c_dev = features.shape
    n_rows = cotangent.shape[0]
    r_dev = n_rows * n_nbr
    scale = (12.0 / (c_dev * n_nbr / 2)) ** 0.5
    row_blocks, col_blocks = r_dev // TILE, c_dev // TILE
    swap_core = [(0, 1), (1, 0)]

    rows_poly, cols_poly = (3, 11), (5, 13)
    packed = weight.shape[0] // 2
    both = jnp.concatenate([pack(weight), cotangent.T], axis=0)

    bases = jnp.stack([nbr_id * c_dev, core * r_dev]).astype(i32)
    partial = edge_product(
        bases, count, pairs, features, row_blocks, col_blocks, False, cols_poly, rows_poly, scale, width
    )
    both, partial = lax.optimization_barrier((both, partial))
    both_z = lax.all_gather(both, "zh")
    partial, both_z = lax.optimization_barrier((exchange(partial, nbr), both_z))
    hidden = jnp.sum(partial, axis=0)
    weight_z = both_z[:, :packed].reshape(-1, TILE)
    hidden, weight_z = lax.optimization_barrier((hidden, copies(weight_z, n_nbr)))
    own = exchange(weight_z, nbr)
    hidden_z = lax.all_gather(hidden, "zh", axis=0, tiled=True)
    hidden_z, own = lax.optimization_barrier((hidden_z, own))
    other = lax.ppermute(own, "core", swap_core)
    hidden_all = lax.all_gather(hidden_z, "x", axis=0, tiled=True)

    at = jnp.stack([core, lax.axis_index("zh")]).astype(i32)
    activations, grad_terms, own_terms, other_terms = layer(
        at, hidden_all, own, other, both_z, n_x, n_zh, weight.shape[0]
    )
    other_terms = lax.ppermute(other_terms, "core", swap_core)
    grad_terms = exchange(grad_terms, "x")
    grad_block = exchange(join(grad_terms, own_terms, other_terms), nbr)
    column_part, weight_grad = edge_product(
        bases[::-1], count, pairs, grad_block, col_blocks, row_blocks, True, rows_poly, cols_poly, scale, width
    )
    feature_grad = column_part + lax.ppermute(column_part, "core", swap_core)
    return activations.T, feature_grad, weight_grad


def halves(n):
    minor = 1
    while minor * minor < n:
        minor *= 2
    return n // minor, minor


def solution(mesh):
    sizes = (mesh.shape["row"], *halves(mesh.shape["nbr"]), *halves(mesh.shape["feat"]))
    fine = Mesh(mesh.devices.reshape(sizes), ("core", "zl", "y", "x", "zh"))
    nbr, feat = ("zl", "y"), ("x", "zh")
    rows = ("core", *nbr)
    in_specs = (P(feat, nbr), P("core", nbr, None, None), P("core", nbr), P(rows, feat), P(rows, feat))
    out_specs = (P(rows, feat), P(feat, nbr), P(rows, feat))
    return jax.shard_map(per_device, mesh=fine, in_specs=in_specs, out_specs=out_specs, check_vma=False)
```

```python
import functools

import jax
import jax.numpy as jnp
from jax import lax
from jax.experimental import pallas as pl
from jax.experimental.pallas import tpu as pltpu
from jax.sharding import Mesh
from jax.sharding import PartitionSpec as P

TILE = 128
MODULUS = 32749
INVERSE = 1.0 / MODULUS
WHOLE = 2**32 // MODULUS
PART = 2**32 / MODULUS - WHOLE
TURN = 2.0**32
OFFSET = 64 - 2**31
f32, bf16, i32 = jnp.float32, jnp.bfloat16, jnp.int32


def residue(value):
    quotient = (value.astype(f32) * INVERSE).astype(i32)
    rest = value - quotient * MODULUS
    rest = jnp.where(rest < 0, rest + MODULUS, rest)
    return jnp.where(rest >= MODULUS, rest - MODULUS, rest)


def turns(value):
    rest = residue(value)
    return rest * WHOLE + (rest.astype(f32) * PART + 0.5).astype(i32)


def split(value):
    high = value.astype(bf16)
    return high, (value - high.astype(f32)).astype(bf16)


def pack(value):
    n = value.shape[-2] // 2
    return jnp.concatenate([value[..., :n, :], value[..., n:, :]], axis=-1)


def unpack(value):
    width = value.shape[-1] // 2
    return jnp.concatenate([value[..., :width], value[..., width:]], axis=-2)


def listed_tiles(swap, sub_blocks, count_ref, pairs_ref, tiles):
    slots = pairs_ref.shape[1]
    major, minor = (pairs_ref[1:2, :], pairs_ref[0:1, :]) if swap else (pairs_ref[0:1, :], pairs_ref[1:2, :])
    code = major * sub_blocks + minor
    code = jnp.where(lax.broadcasted_iota(i32, (1, slots), 1) < count_ref[0], code, -1)
    listed = (lax.broadcasted_iota(i32, (tiles, slots), 0) == code).astype(f32)
    return jnp.broadcast_to(jnp.sum(listed, axis=1, keepdims=True), (tiles, TILE))


def sub_turns(sub_base, sub_blocks, sub_poly):
    shape = (TILE, TILE)
    sub = sub_base + TILE * lax.broadcasted_iota(i32, shape, 0) + lax.broadcasted_iota(i32, shape, 1)
    columns = turns(sub * residue(sub_poly[0] * sub + sub_poly[1])).T
    return [jnp.broadcast_to(columns[:, l:l + 1], shape) for l in range(sub_blocks)]


def lane_turns(j, sub_base, lane_base, sub_blocks, lane_poly):
    lane = lane_base + j * TILE + lax.broadcasted_iota(i32, (sub_blocks, TILE), 1)
    first = sub_base + TILE * lax.broadcasted_iota(i32, (sub_blocks, TILE), 0)
    inner = residue(lane_poly[0] * lane + lane_poly[1] + 7 * first)
    return turns(lane * inner) + OFFSET


def step_turns(lane_base):
    lane = lane_base + lax.broadcasted_iota(i32, (TILE, TILE), 1)
    k = lax.broadcasted_iota(i32, (TILE, TILE), 0)
    return turns(7 * k * lane), turns(7 * TILE * k)


def fold(total, scale):
    width = total.shape[0] // 2
    total = total[:, :TILE] + total[:, TILE:]
    return (total[:width] + total[width:]) * scale


def product_kernel(
    lane_blocks, sub_blocks, swap, sub_poly, lane_poly, scale, width,
    base_ref, count_ref, pairs_ref, source_ref, out_ref, *refs,
):
    sub_table, step_table, growth_table, lane_table, mask_table, source_parts = refs[-6:]
    sub_base, lane_base = base_ref[0], base_ref[1]
    mask_table[...] = listed_tiles(swap, sub_blocks, count_ref, pairs_ref, lane_blocks * sub_blocks)
    for l, table in enumerate(sub_turns(sub_base, sub_blocks, sub_poly)):
        columns = slice(l * TILE, (l + 1) * TILE)
        sub_table[columns, :] = table
        piece = source_ref[l, :width, :] if swap else source_ref[:, columns]
        source_parts[:width, columns], source_parts[width:, columns] = split(piece)
    if swap:
        refs[0][...] = unpack(jnp.sum(source_ref[:, width:, :], axis=0))

    step_table[...], growth_table[...] = step_turns(lane_base)

    def block(j, carry):
        lane_table[...] = lane_turns(j, sub_base, lane_base, sub_blocks, lane_poly)
        total = jnp.zeros((2 * width, 2 * TILE), f32)
        for l in range(0, sub_blocks, 2):
            lhs, rhs = [], []
            for at in (l, l + 1):
                columns = slice(at * TILE, (at + 1) * TILE)
                turn = sub_table[columns, :] + step_table[...] + lane_table[at:at + 1, :]
                rhs.append(jnp.concatenate(split(turn.astype(f32)), axis=1))
                listed = jnp.broadcast_to(mask_table[pl.ds(j * sub_blocks + at, 1), :], (2 * width, TILE)).astype(bf16)
                lhs.append(source_parts[:, columns] * listed)
            total += jnp.dot(
                jnp.concatenate(lhs, axis=1), jnp.concatenate(rhs, axis=0), preferred_element_type=f32
            )
        step_table[...] += growth_table[...]
        result = fold(total, scale / TURN)
        if swap:
            out_ref[:, pl.ds(pl.multiple_of(j * TILE, TILE), TILE)] = result
        else:
            out_ref[j] = result
        return carry

    lax.fori_loop(0, lane_blocks, block, 0, unroll=4)


SMEM, VMEM = pl.BlockSpec(memory_space=pltpu.SMEM), pl.BlockSpec(memory_space=pltpu.VMEM)


def cost(flops, traffic):
    return pl.CostEstimate(flops=flops, bytes_accessed=traffic, transcendentals=0)


def edge_product(base, count, pairs, source, lane_blocks, sub_blocks, swap, sub_poly, lane_poly, scale, width):
    out = jax.ShapeDtypeStruct((lane_blocks, width, TILE), f32)
    if swap:
        out = (
            jax.ShapeDtypeStruct((width, lane_blocks * TILE), f32),
            jax.ShapeDtypeStruct((2 * (source.shape[1] - width), TILE // 2), f32),
        )
    return pl.pallas_call(
        functools.partial(product_kernel, lane_blocks, sub_blocks, swap, sub_poly, lane_poly, scale, width),
        out_shape=out,
        in_specs=[SMEM, SMEM, VMEM, VMEM],
        out_specs=(VMEM, VMEM) if swap else VMEM,
        scratch_shapes=[
            pltpu.VMEM((sub_blocks * TILE, TILE), i32),
            pltpu.VMEM((TILE, TILE), i32),
            pltpu.VMEM((TILE, TILE), i32),
            pltpu.VMEM((sub_blocks, TILE), i32),
            pltpu.VMEM((lane_blocks * sub_blocks, TILE), f32),
            pltpu.VMEM((2 * width, sub_blocks * TILE), bf16),
        ],
        compiler_params=pltpu.CompilerParams(vmem_limit_bytes=24 << 20),
        cost_estimate=cost(8 << 30, 1 << 21),
    )(base, count, pairs, source)


def dot3(a, b):
    a_high, a_low = split(a)
    b_high, b_low = split(b)
    product = functools.partial(jnp.dot, preferred_element_type=f32)
    return product(a_high, b_high) + (product(a_high, b_low) + product(a_low, b_high))


def beside(values):
    return jnp.concatenate(values, axis=-1)


def layer_kernel(
    n_x, n_zh, at_ref, hidden_ref, own_ref, other_ref, both_ref,
    act_ref, grad_ref, own_terms_ref, other_terms_ref, weight,
):
    core, zh = at_ref[0], at_ref[1]
    half = own_ref.shape[0]
    packed, rows, width = own_terms_ref.shape[1], 2 * own_terms_ref.shape[1], own_ref.shape[2] // 2
    depth = hidden_ref.shape[0]
    for which, ref in ((core, own_ref), (1 - core, other_ref)):
        for z in range(0, n_zh, 2):
            pair = [ref[:, at * packed:(at + 1) * packed, :] for at in (z, z + 1)]
            wide = [beside([p[..., :width] for p in pair]), beside([p[..., width:] for p in pair])]
            wide = jnp.concatenate(wide, axis=1).reshape(half * rows, 2 * width)
            weight[pl.ds(pl.multiple_of(which * half * rows, 8), half * rows), z * width:(z + 2) * width] = wide
    cotangent = jnp.concatenate([both_ref[z, width + packed:, :] for z in range(n_zh)], axis=0).T

    pre = dot3(hidden_ref[...].T, weight[...])
    squash = 1.0 / (1.0 + jnp.exp(-pre))
    activations = (pre * squash).T
    grad_pre = cotangent * squash * (1.0 + pre * (1.0 - squash))
    n_rows = pre.shape[0]
    picked = [weight[pl.ds(pl.multiple_of((x * n_zh + zh) * width, 8), width), :] for x in range(n_x)]
    grad_ref[...] = dot3(jnp.concatenate(picked, axis=0), grad_pre.T).reshape(n_x, width, n_rows)

    for z in range(n_zh):
        columns = slice(z * width, (z + 1) * width)

        @pl.when(zh == z)
        def _():
            act_ref[...] = activations[columns, :]
            for which, ref in ((core, own_terms_ref), (1 - core, other_terms_ref)):
                part = hidden_ref[pl.ds(pl.multiple_of(which * (depth // 2), 8), depth // 2), :]
                ref[...] = pack(dot3(part, grad_pre[:, columns]).reshape(half, rows, width))


def layer(at, hidden_all, own, other, both, n_x, n_zh, rows):
    half = own.shape[0]
    width = own.shape[2] // 2
    n_rows = hidden_all.shape[1]
    terms = jax.ShapeDtypeStruct((half, rows // 2, 2 * width), f32)
    return pl.pallas_call(
        functools.partial(layer_kernel, n_x, n_zh),
        out_shape=(
            jax.ShapeDtypeStruct((width, n_rows), f32),
            jax.ShapeDtypeStruct((n_x, width, n_rows), f32),
            terms, terms,
        ),
        in_specs=[SMEM, VMEM, VMEM, VMEM, VMEM],
        out_specs=(VMEM, VMEM, VMEM, VMEM),
        scratch_shapes=[pltpu.VMEM((2 * half * rows, n_zh * width), f32)],
        compiler_params=pltpu.CompilerParams(vmem_limit_bytes=32 << 20),
        cost_estimate=cost(1 << 30, 1 << 21),
    )(at, hidden_all, own, other, both)


def join_kernel(grad_ref, own_ref, other_ref, out_ref):
    width = grad_ref.shape[1]
    grad = jnp.sum(grad_ref[...], axis=0)
    for n in range(out_ref.shape[0]):
        out_ref[n, :width, :] = grad
    out_ref[:, width:, :] = own_ref[...] + other_ref[...]


def join(grad_terms, own_terms, other_terms):
    n, packed, lanes = own_terms.shape
    return pl.pallas_call(
        join_kernel,
        out_shape=jax.ShapeDtypeStruct((n, grad_terms.shape[1] + packed, lanes), f32),
        in_specs=[VMEM] * 3,
        out_specs=VMEM,
        cost_estimate=cost(1 << 20, 1 << 20),
    )(grad_terms, own_terms, other_terms)


def sum_kernel(parts_ref, weight_ref, turned_ref, out_ref):
    width, packed = parts_ref.shape[1], weight_ref.shape[0] // 2
    out_ref[:width, :] = jnp.sum(parts_ref[...], axis=0)
    out_ref[width:width + packed, :] = pack(weight_ref[...])
    out_ref[width + packed:, :] = turned_ref[...]


def sum_parts(parts, weight, turned):
    rows = parts.shape[1] + weight.shape[0] // 2 + turned.shape[0]
    return pl.pallas_call(
        sum_kernel,
        out_shape=jax.ShapeDtypeStruct((rows, parts.shape[2]), f32),
        in_specs=[VMEM] * 3,
        out_specs=VMEM,
        cost_estimate=cost(1 << 20, 1 << 20),
    )(parts, weight, turned)


def deal_kernel(gathered_ref, hidden_ref, weight_ref):
    n_zh = gathered_ref.shape[0]
    width, packed = hidden_ref.shape[0] // n_zh, weight_ref.shape[1] // n_zh
    for z in range(n_zh):
        hidden_ref[z * width:(z + 1) * width, :] = gathered_ref[z, :width, :]
        weight = gathered_ref[z, width:width + packed, :]
        for n in range(weight_ref.shape[0]):
            weight_ref[n, z * packed:(z + 1) * packed, :] = weight


def deal(gathered, width, packed, n):
    n_zh, _, lanes = gathered.shape
    return pl.pallas_call(
        deal_kernel,
        out_shape=(
            jax.ShapeDtypeStruct((n_zh * width, lanes), f32),
            jax.ShapeDtypeStruct((n, n_zh * packed, lanes), f32),
        ),
        in_specs=[VMEM],
        out_specs=(VMEM, VMEM),
        cost_estimate=cost(1 << 20, 1 << 20),
    )(gathered)


def exchange(value, axes):
    return lax.all_to_all(value, axes, 0, 0)


def per_device(features, tile_list, tile_count, weight, cotangent):
    nbr, feat = ("zl", "y"), ("x", "zh")
    pairs, count = tile_list[0, 0], tile_count[0]
    n_nbr = lax.axis_size(nbr)
    n_x, n_zh = lax.axis_size("x"), lax.axis_size("zh")
    core, nbr_id = lax.axis_index("core"), lax.axis_index(nbr)
    width, c_dev = features.shape
    n_rows = cotangent.shape[0]
    r_dev = n_rows * n_nbr
    scale = (12.0 / (c_dev * n_nbr / 2)) ** 0.5
    row_blocks, col_blocks = r_dev // TILE, c_dev // TILE
    swap_core = [(0, 1), (1, 0)]

    rows_poly, cols_poly = (3, 11), (5, 13)
    packed = weight.shape[0] // 2
    bases = jnp.stack([nbr_id * c_dev, core * r_dev]).astype(i32)
    partial = edge_product(
        bases, count, pairs, features, row_blocks, col_blocks, False, cols_poly, rows_poly, scale, width
    )
    gathered = lax.all_gather(sum_parts(exchange(partial, nbr), weight, cotangent.T), "zh")
    hidden_z, weight_z = deal(gathered, width, packed, n_nbr)
    own = exchange(weight_z, nbr)
    hidden_all = lax.all_gather(hidden_z, "x", axis=0, tiled=True)
    hidden_all, own = lax.optimization_barrier((hidden_all, own))
    other = lax.ppermute(own, "core", swap_core)

    at = jnp.stack([core, lax.axis_index("zh")]).astype(i32)
    activations, grad_terms, own_terms, other_terms = layer(
        at, hidden_all, own, other, gathered, n_x, n_zh, weight.shape[0]
    )
    other_terms = lax.ppermute(other_terms, "core", swap_core)
    grad_terms = exchange(grad_terms, "x")
    grad_block = exchange(join(grad_terms, own_terms, other_terms), nbr)
    column_part, weight_grad = edge_product(
        bases[::-1], count, pairs, grad_block, col_blocks, row_blocks, True, rows_poly, cols_poly, scale, width
    )
    feature_grad = column_part + lax.ppermute(column_part, "core", swap_core)
    return activations.T, feature_grad, weight_grad


def halves(n):
    minor = 1
    while minor * minor < n:
        minor *= 2
    return n // minor, minor


def solution(mesh):
    sizes = (mesh.shape["row"], *halves(mesh.shape["nbr"]), *halves(mesh.shape["feat"]))
    fine = Mesh(mesh.devices.reshape(sizes), ("core", "zl", "y", "x", "zh"))
    nbr, feat = ("zl", "y"), ("x", "zh")
    rows = ("core", *nbr)
    in_specs = (P(feat, nbr), P("core", nbr, None, None), P("core", nbr), P(rows, feat), P(rows, feat))
    out_specs = (P(rows, feat), P(feat, nbr), P(rows, feat))
    return jax.shard_map(per_device, mesh=fine, in_specs=in_specs, out_specs=out_specs, check_vma=False)
```

```python
import functools

import jax
import jax.numpy as jnp
from jax import lax
from jax.experimental import pallas as pl
from jax.experimental.pallas import tpu as pltpu
from jax.sharding import Mesh
from jax.sharding import PartitionSpec as P

TILE = 128
MODULUS = 32749
INVERSE = 1.0 / MODULUS
WHOLE = 2**32 // MODULUS
PART = 2**32 / MODULUS - WHOLE
TURN = 2.0**32
OFFSET = 64 - 2**31
f32, bf16, i32 = jnp.float32, jnp.bfloat16, jnp.int32


def residue(value):
    quotient = (value.astype(f32) * INVERSE).astype(i32)
    rest = value - quotient * MODULUS
    rest = jnp.where(rest < 0, rest + MODULUS, rest)
    return jnp.where(rest >= MODULUS, rest - MODULUS, rest)


def turns(value):
    rest = residue(value)
    return rest * WHOLE + (rest.astype(f32) * PART + 0.5).astype(i32)


def split(value):
    high = value.astype(bf16)
    return high, (value - high.astype(f32)).astype(bf16)


def pack(value):
    n = value.shape[-2] // 2
    return jnp.concatenate([value[..., :n, :], value[..., n:, :]], axis=-1)


def unpack(value):
    width = value.shape[-1] // 2
    return jnp.concatenate([value[..., :width], value[..., width:]], axis=-2)


def listed_tiles(swap, sub_blocks, count_ref, pairs_ref, tiles):
    slots = pairs_ref.shape[1]
    major, minor = (pairs_ref[1:2, :], pairs_ref[0:1, :]) if swap else (pairs_ref[0:1, :], pairs_ref[1:2, :])
    code = major * sub_blocks + minor
    code = jnp.where(lax.broadcasted_iota(i32, (1, slots), 1) < count_ref[0], code, -1)
    listed = (lax.broadcasted_iota(i32, (tiles, slots), 0) == code).astype(f32)
    return jnp.broadcast_to(jnp.sum(listed, axis=1, keepdims=True), (tiles, TILE))


def sub_turns(sub_base, sub_blocks, sub_poly):
    shape = (TILE, TILE)
    sub = sub_base + TILE * lax.broadcasted_iota(i32, shape, 0) + lax.broadcasted_iota(i32, shape, 1)
    columns = turns(sub * residue(sub_poly[0] * sub + sub_poly[1])).T
    return [jnp.broadcast_to(columns[:, l:l + 1], shape) for l in range(sub_blocks)]


def lane_turns(j, sub_base, lane_base, sub_blocks, lane_poly):
    lane = lane_base + j * TILE + lax.broadcasted_iota(i32, (sub_blocks, TILE), 1)
    first = sub_base + TILE * lax.broadcasted_iota(i32, (sub_blocks, TILE), 0)
    inner = residue(lane_poly[0] * lane + lane_poly[1] + 7 * first)
    return turns(lane * inner) + OFFSET


def step_turns(lane_base):
    lane = lane_base + lax.broadcasted_iota(i32, (TILE, TILE), 1)
    k = lax.broadcasted_iota(i32, (TILE, TILE), 0)
    return turns(7 * k * lane), turns(7 * TILE * k)


def fold(total, scale):
    width = total.shape[0] // 2
    total = total[:, :TILE] + total[:, TILE:]
    return (total[:width] + total[width:]) * scale


def product_kernel(
    lane_blocks, sub_blocks, swap, sub_poly, lane_poly, scale, width,
    base_ref, count_ref, pairs_ref, source_ref, out_ref, *refs,
):
    sub_table, step_table, growth_table, lane_table, mask_table, source_parts = refs[-6:]
    sub_base, lane_base = base_ref[0], base_ref[1]
    mask_table[...] = listed_tiles(swap, sub_blocks, count_ref, pairs_ref, lane_blocks * sub_blocks)
    for l, table in enumerate(sub_turns(sub_base, sub_blocks, sub_poly)):
        columns = slice(l * TILE, (l + 1) * TILE)
        sub_table[columns, :] = table
        piece = source_ref[l, :width, :] if swap else source_ref[:, columns]
        source_parts[:width, columns], source_parts[width:, columns] = split(piece)
    if swap:
        refs[0][...] = unpack(jnp.sum(source_ref[:, width:, :], axis=0))

    step_table[...], growth_table[...] = step_turns(lane_base)

    def block(j, carry):
        lane_table[...] = lane_turns(j, sub_base, lane_base, sub_blocks, lane_poly)
        total = jnp.zeros((2 * width, 2 * TILE), f32)
        for l in range(0, sub_blocks, 2):
            lhs, rhs = [], []
            for at in (l, l + 1):
                columns = slice(at * TILE, (at + 1) * TILE)
                turn = sub_table[columns, :] + step_table[...] + lane_table[at:at + 1, :]
                rhs.append(jnp.concatenate(split(turn.astype(f32)), axis=1))
                listed = jnp.broadcast_to(mask_table[pl.ds(j * sub_blocks + at, 1), :], (2 * width, TILE)).astype(bf16)
                lhs.append(source_parts[:, columns] * listed)
            total += jnp.dot(
                jnp.concatenate(lhs, axis=1), jnp.concatenate(rhs, axis=0), preferred_element_type=f32
            )
        step_table[...] += growth_table[...]
        result = fold(total, scale / TURN)
        if swap:
            out_ref[:, pl.ds(pl.multiple_of(j * TILE, TILE), TILE)] = result
        else:
            out_ref[j] = result
        return carry

    lax.fori_loop(0, lane_blocks, block, 0, unroll=4)


SMEM, VMEM = pl.BlockSpec(memory_space=pltpu.SMEM), pl.BlockSpec(memory_space=pltpu.VMEM)


def cost(flops, traffic):
    return pl.CostEstimate(flops=flops, bytes_accessed=traffic, transcendentals=0)


def edge_product(base, count, pairs, source, lane_blocks, sub_blocks, swap, sub_poly, lane_poly, scale, width):
    out = jax.ShapeDtypeStruct((lane_blocks, width, TILE), f32)
    if swap:
        out = (
            jax.ShapeDtypeStruct((width, lane_blocks * TILE), f32),
            jax.ShapeDtypeStruct((2 * (source.shape[1] - width), TILE // 2), f32),
        )
    return pl.pallas_call(
        functools.partial(product_kernel, lane_blocks, sub_blocks, swap, sub_poly, lane_poly, scale, width),
        out_shape=out,
        in_specs=[SMEM, SMEM, VMEM, VMEM],
        out_specs=(VMEM, VMEM) if swap else VMEM,
        scratch_shapes=[
            pltpu.VMEM((sub_blocks * TILE, TILE), i32),
            pltpu.VMEM((TILE, TILE), i32),
            pltpu.VMEM((TILE, TILE), i32),
            pltpu.VMEM((sub_blocks, TILE), i32),
            pltpu.VMEM((lane_blocks * sub_blocks, TILE), f32),
            pltpu.VMEM((2 * width, sub_blocks * TILE), bf16),
        ],
        compiler_params=pltpu.CompilerParams(vmem_limit_bytes=24 << 20),
        cost_estimate=cost(8 << 30, 1 << 21),
    )(base, count, pairs, source)


def dot3(a, b):
    a_high, a_low = split(a)
    b_high, b_low = split(b)
    product = functools.partial(jnp.dot, preferred_element_type=f32)
    return product(a_high, b_high) + (product(a_high, b_low) + product(a_low, b_high))


def beside(values):
    return jnp.concatenate(values, axis=-1)


def layer_kernel(
    n_x, n_zh, at_ref, hidden_ref, own_ref, other_ref, both_ref,
    act_ref, grad_ref, own_terms_ref, other_terms_ref, weight,
):
    core, zh = at_ref[0], at_ref[1]
    half = own_ref.shape[0]
    packed, rows, width = own_terms_ref.shape[1], 2 * own_terms_ref.shape[1], own_ref.shape[2] // 2
    depth = hidden_ref.shape[0]
    for which, ref in ((core, own_ref), (1 - core, other_ref)):
        for z in range(0, n_zh, 2):
            pair = [ref[:, at * packed:(at + 1) * packed, :] for at in (z, z + 1)]
            wide = [beside([p[..., :width] for p in pair]), beside([p[..., width:] for p in pair])]
            wide = jnp.concatenate(wide, axis=1).reshape(half * rows, 2 * width)
            weight[pl.ds(pl.multiple_of(which * half * rows, 8), half * rows), z * width:(z + 2) * width] = wide
    cotangent = jnp.concatenate([both_ref[z, width + packed:, :] for z in range(n_zh)], axis=0).T

    pre = dot3(hidden_ref[...].T, weight[...])
    squash = 1.0 / (1.0 + jnp.exp(-pre))
    activations = (pre * squash).T
    grad_pre = cotangent * squash * (1.0 + pre * (1.0 - squash))
    n_rows = pre.shape[0]
    picked = [weight[pl.ds(pl.multiple_of((x * n_zh + zh) * width, 8), width), :] for x in range(n_x)]
    grad_ref[...] = dot3(jnp.concatenate(picked, axis=0), grad_pre.T).reshape(n_x, width, n_rows)

    for z in range(n_zh):
        columns = slice(z * width, (z + 1) * width)

        @pl.when(zh == z)
        def _():
            act_ref[...] = activations[columns, :]
            for which, ref in ((core, own_terms_ref), (1 - core, other_terms_ref)):
                part = hidden_ref[pl.ds(pl.multiple_of(which * (depth // 2), 8), depth // 2), :]
                ref[...] = pack(dot3(part, grad_pre[:, columns]).reshape(half, rows, width))


def layer(at, hidden_all, own, other, both, n_x, n_zh, rows):
    half = own.shape[0]
    width = own.shape[2] // 2
    n_rows = hidden_all.shape[1]
    terms = jax.ShapeDtypeStruct((half, rows // 2, 2 * width), f32)
    return pl.pallas_call(
        functools.partial(layer_kernel, n_x, n_zh),
        out_shape=(
            jax.ShapeDtypeStruct((width, n_rows), f32),
            jax.ShapeDtypeStruct((n_x, width, n_rows), f32),
            terms, terms,
        ),
        in_specs=[SMEM, VMEM, VMEM, VMEM, VMEM],
        out_specs=(VMEM, VMEM, VMEM, VMEM),
        scratch_shapes=[pltpu.VMEM((2 * half * rows, n_zh * width), f32)],
        compiler_params=pltpu.CompilerParams(vmem_limit_bytes=32 << 20),
        cost_estimate=cost(1 << 30, 1 << 21),
    )(at, hidden_all, own, other, both)


def join_kernel(grad_ref, own_ref, other_ref, out_ref):
    width = grad_ref.shape[1]
    grad = jnp.sum(grad_ref[...], axis=0)
    for n in range(out_ref.shape[0]):
        out_ref[n, :width, :] = grad
    out_ref[:, width:, :] = own_ref[...] + other_ref[...]


def join(grad_terms, own_terms, other_terms):
    n, packed, lanes = own_terms.shape
    return pl.pallas_call(
        join_kernel,
        out_shape=jax.ShapeDtypeStruct((n, grad_terms.shape[1] + packed, lanes), f32),
        in_specs=[VMEM] * 3,
        out_specs=VMEM,
        cost_estimate=cost(1 << 20, 1 << 20),
    )(grad_terms, own_terms, other_terms)


def sum_kernel(parts_ref, weight_ref, turned_ref, out_ref):
    width, packed = parts_ref.shape[1], weight_ref.shape[0] // 2
    total = jnp.sum(parts_ref[...], axis=0)
    weight = pack(weight_ref[...])
    for n in range(out_ref.shape[0]):
        out_ref[n, :width, :] = total
        out_ref[n, width:width + packed, :] = weight
        out_ref[n, width + packed:, :] = turned_ref[...]


def sum_parts(parts, weight, turned, n):
    rows = parts.shape[1] + weight.shape[0] // 2 + turned.shape[0]
    return pl.pallas_call(
        sum_kernel,
        out_shape=jax.ShapeDtypeStruct((n, rows, parts.shape[2]), f32),
        in_specs=[VMEM] * 3,
        out_specs=VMEM,
        cost_estimate=cost(1 << 20, 1 << 20),
    )(parts, weight, turned)


def deal_kernel(gathered_ref, hidden_ref, weight_ref):
    n_zh = gathered_ref.shape[0]
    width, packed = hidden_ref.shape[0] // n_zh, weight_ref.shape[1] // n_zh
    for z in range(n_zh):
        hidden_ref[z * width:(z + 1) * width, :] = gathered_ref[z, :width, :]
        weight = gathered_ref[z, width:width + packed, :]
        for n in range(weight_ref.shape[0]):
            weight_ref[n, z * packed:(z + 1) * packed, :] = weight


def deal(gathered, width, packed, n):
    n_zh, _, lanes = gathered.shape
    return pl.pallas_call(
        deal_kernel,
        out_shape=(
            jax.ShapeDtypeStruct((n_zh * width, lanes), f32),
            jax.ShapeDtypeStruct((n, n_zh * packed, lanes), f32),
        ),
        in_specs=[VMEM],
        out_specs=(VMEM, VMEM),
        cost_estimate=cost(1 << 20, 1 << 20),
    )(gathered)


def exchange(value, axes):
    return lax.all_to_all(value, axes, 0, 0)


def per_device(features, tile_list, tile_count, weight, cotangent):
    nbr, feat = ("zl", "y"), ("x", "zh")
    pairs, count = tile_list[0, 0], tile_count[0]
    n_nbr = lax.axis_size(nbr)
    n_x, n_zh = lax.axis_size("x"), lax.axis_size("zh")
    core, nbr_id = lax.axis_index("core"), lax.axis_index(nbr)
    width, c_dev = features.shape
    n_rows = cotangent.shape[0]
    r_dev = n_rows * n_nbr
    scale = (12.0 / (c_dev * n_nbr / 2)) ** 0.5
    row_blocks, col_blocks = r_dev // TILE, c_dev // TILE
    swap_core = [(0, 1), (1, 0)]

    rows_poly, cols_poly = (3, 11), (5, 13)
    packed = weight.shape[0] // 2
    bases = jnp.stack([nbr_id * c_dev, core * r_dev]).astype(i32)
    partial = edge_product(
        bases, count, pairs, features, row_blocks, col_blocks, False, cols_poly, rows_poly, scale, width
    )
    gathered = exchange(sum_parts(exchange(partial, nbr), weight, cotangent.T, n_zh), "zh")
    hidden_z, weight_z = deal(gathered, width, packed, n_nbr)
    own = exchange(weight_z, nbr)
    hidden_all = lax.all_gather(hidden_z, "x", axis=0, tiled=True)
    hidden_all, own = lax.optimization_barrier((hidden_all, own))
    other = lax.ppermute(own, "core", swap_core)

    at = jnp.stack([core, lax.axis_index("zh")]).astype(i32)
    activations, grad_terms, own_terms, other_terms = layer(
        at, hidden_all, own, other, gathered, n_x, n_zh, weight.shape[0]
    )
    other_terms = lax.ppermute(other_terms, "core", swap_core)
    grad_terms = exchange(grad_terms, "x")
    grad_block = exchange(join(grad_terms, own_terms, other_terms), nbr)
    column_part, weight_grad = edge_product(
        bases[::-1], count, pairs, grad_block, col_blocks, row_blocks, True, rows_poly, cols_poly, scale, width
    )
    feature_grad = column_part + lax.ppermute(column_part, "core", swap_core)
    return activations.T, feature_grad, weight_grad


def halves(n):
    minor = 1
    while minor * minor < n:
        minor *= 2
    return n // minor, minor


def solution(mesh):
    sizes = (mesh.shape["row"], *halves(mesh.shape["nbr"]), *halves(mesh.shape["feat"]))
    fine = Mesh(mesh.devices.reshape(sizes), ("core", "zl", "y", "x", "zh"))
    nbr, feat = ("zl", "y"), ("x", "zh")
    rows = ("core", *nbr)
    in_specs = (P(feat, nbr), P("core", nbr, None, None), P("core", nbr), P(rows, feat), P(rows, feat))
    out_specs = (P(rows, feat), P(feat, nbr), P(rows, feat))
    return jax.shard_map(per_device, mesh=fine, in_specs=in_specs, out_specs=out_specs, check_vma=False)
```

```python
import functools

import jax
import jax.numpy as jnp
from jax import lax
from jax.experimental import pallas as pl
from jax.experimental.pallas import tpu as pltpu
from jax.sharding import Mesh
from jax.sharding import PartitionSpec as P

TILE = 128
MODULUS = 32749
INVERSE = 1.0 / MODULUS
WHOLE = 2**32 // MODULUS
PART = 2**32 / MODULUS - WHOLE
TURN = 2.0**32
OFFSET = 64 - 2**31
f32, bf16, i32 = jnp.float32, jnp.bfloat16, jnp.int32


def residue(value):
    quotient = (value.astype(f32) * INVERSE).astype(i32)
    rest = value - quotient * MODULUS
    rest = jnp.where(rest < 0, rest + MODULUS, rest)
    return jnp.where(rest >= MODULUS, rest - MODULUS, rest)


def turns(value):
    rest = residue(value)
    return rest * WHOLE + (rest.astype(f32) * PART + 0.5).astype(i32)


def split(value):
    high = value.astype(bf16)
    return high, (value - high.astype(f32)).astype(bf16)


def pack(value):
    n = value.shape[-2] // 2
    return jnp.concatenate([value[..., :n, :], value[..., n:, :]], axis=-1)


def unpack(value):
    width = value.shape[-1] // 2
    return jnp.concatenate([value[..., :width], value[..., width:]], axis=-2)


def listed_tiles(swap, sub_blocks, count_ref, pairs_ref, tiles):
    slots = pairs_ref.shape[1]
    major, minor = (pairs_ref[1:2, :], pairs_ref[0:1, :]) if swap else (pairs_ref[0:1, :], pairs_ref[1:2, :])
    code = major * sub_blocks + minor
    code = jnp.where(lax.broadcasted_iota(i32, (1, slots), 1) < count_ref[0], code, -1)
    listed = (lax.broadcasted_iota(i32, (tiles, slots), 0) == code).astype(f32)
    return jnp.broadcast_to(jnp.sum(listed, axis=1, keepdims=True), (tiles, TILE))


def sub_turns(sub_base, sub_blocks, sub_poly):
    shape = (TILE, TILE)
    sub = sub_base + TILE * lax.broadcasted_iota(i32, shape, 0) + lax.broadcasted_iota(i32, shape, 1)
    columns = turns(sub * residue(sub_poly[0] * sub + sub_poly[1])).T
    return [jnp.broadcast_to(columns[:, l:l + 1], shape) for l in range(sub_blocks)]


def lane_turns(j, sub_base, lane_base, sub_blocks, lane_poly):
    lane = lane_base + j * TILE + lax.broadcasted_iota(i32, (sub_blocks, TILE), 1)
    first = sub_base + TILE * lax.broadcasted_iota(i32, (sub_blocks, TILE), 0)
    inner = residue(lane_poly[0] * lane + lane_poly[1] + 7 * first)
    return turns(lane * inner) + OFFSET


def step_turns(lane_base):
    lane = lane_base + lax.broadcasted_iota(i32, (TILE, TILE), 1)
    k = lax.broadcasted_iota(i32, (TILE, TILE), 0)
    return turns(7 * k * lane), turns(7 * TILE * k)


def fold(total, scale):
    width = total.shape[0] // 2
    total = total[:, :TILE] + total[:, TILE:]
    return (total[:width] + total[width:]) * scale


def product_kernel(
    lane_blocks, sub_blocks, swap, sub_poly, lane_poly, scale, width,
    base_ref, count_ref, pairs_ref, source_ref, out_ref, *refs,
):
    sub_table, step_table, growth_table, lane_table, mask_table, source_parts = refs[-6:]
    sub_base, lane_base = base_ref[0], base_ref[1]
    mask_table[...] = listed_tiles(swap, sub_blocks, count_ref, pairs_ref, lane_blocks * sub_blocks)
    for l, table in enumerate(sub_turns(sub_base, sub_blocks, sub_poly)):
        columns = slice(l * TILE, (l + 1) * TILE)
        sub_table[columns, :] = table
        piece = source_ref[l, :width, :] if swap else source_ref[:, columns]
        source_parts[:width, columns], source_parts[width:, columns] = split(piece)
    if swap:
        refs[0][...] = unpack(jnp.sum(source_ref[:, width:, :], axis=0))

    step_table[...], growth_table[...] = step_turns(lane_base)

    def block(j, carry):
        lane_table[...] = lane_turns(j, sub_base, lane_base, sub_blocks, lane_poly)
        total = jnp.zeros((2 * width, 2 * TILE), f32)
        for l in range(0, sub_blocks, 2):
            lhs, rhs = [], []
            for at in (l, l + 1):
                columns = slice(at * TILE, (at + 1) * TILE)
                turn = sub_table[columns, :] + step_table[...] + lane_table[at:at + 1, :]
                rhs.append(jnp.concatenate(split(turn.astype(f32)), axis=1))
                listed = jnp.broadcast_to(mask_table[pl.ds(j * sub_blocks + at, 1), :], (2 * width, TILE)).astype(bf16)
                lhs.append(source_parts[:, columns] * listed)
            total += jnp.dot(
                jnp.concatenate(lhs, axis=1), jnp.concatenate(rhs, axis=0), preferred_element_type=f32
            )
        step_table[...] += growth_table[...]
        result = fold(total, scale / TURN)
        if swap:
            out_ref[:, pl.ds(pl.multiple_of(j * TILE, TILE), TILE)] = result
        else:
            out_ref[j] = result
        return carry

    lax.fori_loop(0, lane_blocks, block, 0, unroll=4)


SMEM, VMEM = pl.BlockSpec(memory_space=pltpu.SMEM), pl.BlockSpec(memory_space=pltpu.VMEM)


def cost(flops, traffic):
    return pl.CostEstimate(flops=flops, bytes_accessed=traffic, transcendentals=0)


def edge_product(base, count, pairs, source, lane_blocks, sub_blocks, swap, sub_poly, lane_poly, scale, width):
    out = jax.ShapeDtypeStruct((lane_blocks, width, TILE), f32)
    if swap:
        out = (
            jax.ShapeDtypeStruct((width, lane_blocks * TILE), f32),
            jax.ShapeDtypeStruct((2 * (source.shape[1] - width), TILE // 2), f32),
        )
    return pl.pallas_call(
        functools.partial(product_kernel, lane_blocks, sub_blocks, swap, sub_poly, lane_poly, scale, width),
        out_shape=out,
        in_specs=[SMEM, SMEM, VMEM, VMEM],
        out_specs=(VMEM, VMEM) if swap else VMEM,
        scratch_shapes=[
            pltpu.VMEM((sub_blocks * TILE, TILE), i32),
            pltpu.VMEM((TILE, TILE), i32),
            pltpu.VMEM((TILE, TILE), i32),
            pltpu.VMEM((sub_blocks, TILE), i32),
            pltpu.VMEM((lane_blocks * sub_blocks, TILE), f32),
            pltpu.VMEM((2 * width, sub_blocks * TILE), bf16),
        ],
        compiler_params=pltpu.CompilerParams(vmem_limit_bytes=24 << 20),
        cost_estimate=cost(8 << 30, 1 << 21),
    )(base, count, pairs, source)


def dot3(a, b):
    a_high, a_low = split(a)
    b_high, b_low = split(b)
    product = functools.partial(jnp.dot, preferred_element_type=f32)
    return product(a_high, b_high) + (product(a_high, b_low) + product(a_low, b_high))


def beside(values):
    return jnp.concatenate(values, axis=-1)


def layer_kernel(
    n_x, n_zh, at_ref, hidden_ref, own_ref, other_ref, both_ref,
    act_ref, grad_ref, own_terms_ref, other_terms_ref, weight,
):
    core, zh = at_ref[0], at_ref[1]
    half = own_ref.shape[0]
    packed, rows, width = own_terms_ref.shape[1], 2 * own_terms_ref.shape[1], own_ref.shape[2] // 2
    depth = hidden_ref.shape[0]
    for which, ref in ((core, own_ref), (1 - core, other_ref)):
        for z in range(0, n_zh, 2):
            pair = [ref[:, at * packed:(at + 1) * packed, :] for at in (z, z + 1)]
            wide = [beside([p[..., :width] for p in pair]), beside([p[..., width:] for p in pair])]
            wide = jnp.concatenate(wide, axis=1).reshape(half * rows, 2 * width)
            weight[pl.ds(pl.multiple_of(which * half * rows, 8), half * rows), z * width:(z + 2) * width] = wide
    cotangent = jnp.concatenate([both_ref[z, width + packed:, :] for z in range(n_zh)], axis=0).T

    pre = dot3(hidden_ref[...].T, weight[...])
    squash = 1.0 / (1.0 + jnp.exp(-pre))
    activations = (pre * squash).T
    grad_pre = cotangent * squash * (1.0 + pre * (1.0 - squash))
    n_rows = pre.shape[0]
    picked = [weight[pl.ds(pl.multiple_of((x * n_zh + zh) * width, 8), width), :] for x in range(n_x)]
    grad_ref[...] = dot3(jnp.concatenate(picked, axis=0), grad_pre.T).reshape(n_x, width, n_rows)

    for z in range(n_zh):
        columns = slice(z * width, (z + 1) * width)

        @pl.when(zh == z)
        def _():
            act_ref[...] = activations[columns, :]
            for which, ref in ((core, own_terms_ref), (1 - core, other_terms_ref)):
                part = hidden_ref[pl.ds(pl.multiple_of(which * (depth // 2), 8), depth // 2), :]
                ref[...] = pack(dot3(part, grad_pre[:, columns]).reshape(half, rows, width))


def layer(at, hidden_all, own, other, both, n_x, n_zh, rows):
    half = own.shape[0]
    width = own.shape[2] // 2
    n_rows = hidden_all.shape[1]
    terms = jax.ShapeDtypeStruct((half, rows // 2, 2 * width), f32)
    return pl.pallas_call(
        functools.partial(layer_kernel, n_x, n_zh),
        out_shape=(
            jax.ShapeDtypeStruct((width, n_rows), f32),
            jax.ShapeDtypeStruct((n_x, width, n_rows), f32),
            terms, terms,
        ),
        in_specs=[SMEM, VMEM, VMEM, VMEM, VMEM],
        out_specs=(VMEM, VMEM, VMEM, VMEM),
        scratch_shapes=[pltpu.VMEM((2 * half * rows, n_zh * width), f32)],
        compiler_params=pltpu.CompilerParams(vmem_limit_bytes=32 << 20),
        cost_estimate=cost(1 << 30, 1 << 21),
    )(at, hidden_all, own, other, both)


def copies(value, n):
    return jnp.broadcast_to(value[None], (n,) + value.shape)


def exchange(value, axes):
    return lax.all_to_all(value, axes, 0, 0)


def per_device(features, tile_list, tile_count, weight, cotangent):
    nbr, feat = ("zl", "y"), ("x", "zh")
    pairs, count = tile_list[0, 0], tile_count[0]
    n_nbr = lax.axis_size(nbr)
    n_x, n_zh = lax.axis_size("x"), lax.axis_size("zh")
    core, nbr_id = lax.axis_index("core"), lax.axis_index(nbr)
    width, c_dev = features.shape
    n_rows = cotangent.shape[0]
    r_dev = n_rows * n_nbr
    scale = (12.0 / (c_dev * n_nbr / 2)) ** 0.5
    row_blocks, col_blocks = r_dev // TILE, c_dev // TILE
    swap_core = [(0, 1), (1, 0)]

    rows_poly, cols_poly = (3, 11), (5, 13)
    packed = weight.shape[0] // 2
    bases = jnp.stack([nbr_id * c_dev, core * r_dev]).astype(i32)
    partial = edge_product(
        bases, count, pairs, features, row_blocks, col_blocks, False, cols_poly, rows_poly, scale, width
    )
    hidden = jnp.sum(exchange(partial, nbr), axis=0)
    gathered = lax.all_gather(jnp.concatenate([hidden, pack(weight), cotangent.T], axis=0), "zh")
    weight_z = gathered[:, width:width + packed].reshape(-1, TILE)
    hidden_z = gathered[:, :width].reshape(-1, n_rows)
    own = exchange(copies(weight_z, n_nbr), nbr)
    hidden_all = lax.all_gather(hidden_z, "x", axis=0, tiled=True)
    hidden_all, own = lax.optimization_barrier((hidden_all, own))
    other = lax.ppermute(own, "core", swap_core)

    at = jnp.stack([core, lax.axis_index("zh")]).astype(i32)
    activations, grad_terms, own_terms, other_terms = layer(
        at, hidden_all, own, other, gathered, n_x, n_zh, weight.shape[0]
    )
    other_terms = lax.ppermute(other_terms, "core", swap_core)
    grad_terms = exchange(grad_terms, "x")
    grad_hidden = copies(jnp.sum(grad_terms, axis=0), n_nbr)
    grad_block = exchange(jnp.concatenate([grad_hidden, own_terms + other_terms], axis=1), nbr)
    column_part, weight_grad = edge_product(
        bases[::-1], count, pairs, grad_block, col_blocks, row_blocks, True, rows_poly, cols_poly, scale, width
    )
    feature_grad = column_part + lax.ppermute(column_part, "core", swap_core)
    return activations.T, feature_grad, weight_grad


def halves(n):
    minor = 1
    while minor * minor < n:
        minor *= 2
    return n // minor, minor


def solution(mesh):
    sizes = (mesh.shape["row"], *halves(mesh.shape["nbr"]), *halves(mesh.shape["feat"]))
    fine = Mesh(mesh.devices.reshape(sizes), ("core", "zl", "y", "x", "zh"))
    nbr, feat = ("zl", "y"), ("x", "zh")
    rows = ("core", *nbr)
    in_specs = (P(feat, nbr), P("core", nbr, None, None), P("core", nbr), P(rows, feat), P(rows, feat))
    out_specs = (P(rows, feat), P(feat, nbr), P(rows, feat))
    return jax.shard_map(per_device, mesh=fine, in_specs=in_specs, out_specs=out_specs, check_vma=False)
```

```python
import functools

import jax
import jax.numpy as jnp
from jax import lax
from jax.experimental import pallas as pl
from jax.experimental.pallas import tpu as pltpu
from jax.sharding import Mesh
from jax.sharding import PartitionSpec as P

TILE = 128
MODULUS = 32749
INVERSE = 1.0 / MODULUS
WHOLE = 2**32 // MODULUS
PART = 2**32 / MODULUS - WHOLE
TURN = 2.0**32
OFFSET = 64 - 2**31
f32, bf16, i32 = jnp.float32, jnp.bfloat16, jnp.int32


def residue(value):
    quotient = (value.astype(f32) * INVERSE).astype(i32)
    rest = value - quotient * MODULUS
    rest = jnp.where(rest < 0, rest + MODULUS, rest)
    return jnp.where(rest >= MODULUS, rest - MODULUS, rest)


def turns(value):
    rest = residue(value)
    return rest * WHOLE + (rest.astype(f32) * PART + 0.5).astype(i32)


def split(value):
    high = value.astype(bf16)
    return high, (value - high.astype(f32)).astype(bf16)


def pack(value):
    n = value.shape[-2] // 2
    return jnp.concatenate([value[..., :n, :], value[..., n:, :]], axis=-1)


def unpack(value):
    width = value.shape[-1] // 2
    return jnp.concatenate([value[..., :width], value[..., width:]], axis=-2)


def listed_tiles(swap, sub_blocks, count_ref, pairs_ref, tiles):
    slots = pairs_ref.shape[1]
    major, minor = (pairs_ref[1:2, :], pairs_ref[0:1, :]) if swap else (pairs_ref[0:1, :], pairs_ref[1:2, :])
    code = major * sub_blocks + minor
    code = jnp.where(lax.broadcasted_iota(i32, (1, slots), 1) < count_ref[0], code, -1)
    listed = (lax.broadcasted_iota(i32, (tiles, slots), 0) == code).astype(f32)
    return jnp.broadcast_to(jnp.sum(listed, axis=1, keepdims=True), (tiles, TILE))


def sub_turns(sub_base, sub_blocks, sub_poly):
    shape = (TILE, TILE)
    sub = sub_base + TILE * lax.broadcasted_iota(i32, shape, 0) + lax.broadcasted_iota(i32, shape, 1)
    columns = turns(sub * residue(sub_poly[0] * sub + sub_poly[1])).T
    return [jnp.broadcast_to(columns[:, l:l + 1], shape) for l in range(sub_blocks)]


def lane_turns(j, sub_base, lane_base, sub_blocks, lane_poly):
    lane = lane_base + j * TILE + lax.broadcasted_iota(i32, (sub_blocks, TILE), 1)
    first = sub_base + TILE * lax.broadcasted_iota(i32, (sub_blocks, TILE), 0)
    inner = residue(lane_poly[0] * lane + lane_poly[1] + 7 * first)
    return turns(lane * inner) + OFFSET


def step_turns(lane_base):
    lane = lane_base + lax.broadcasted_iota(i32, (TILE, TILE), 1)
    k = lax.broadcasted_iota(i32, (TILE, TILE), 0)
    return turns(7 * k * lane), turns(7 * TILE * k)


def fold(total, scale):
    width = total.shape[0] // 2
    total = total[:, :TILE] + total[:, TILE:]
    return (total[:width] + total[width:]) * scale


def product_kernel(
    lane_blocks, sub_blocks, swap, sub_poly, lane_poly, scale, width,
    base_ref, count_ref, pairs_ref, source_ref, *refs,
):
    sub_table, step_table, growth_table, lane_table, mask_table, source_parts = refs[-6:]
    if not swap:
        out_ref, fetched, arrived = refs[:3]
        fetch = pltpu.make_async_copy(source_ref, fetched, arrived)
        fetch.start()
    sub_base, lane_base = base_ref[0], base_ref[1]
    mask_table[...] = listed_tiles(swap, sub_blocks, count_ref, pairs_ref, lane_blocks * sub_blocks)
    for l, table in enumerate(sub_turns(sub_base, sub_blocks, sub_poly)):
        sub_table[l * TILE:(l + 1) * TILE, :] = table

    step_table[...], growth_table[...] = step_turns(lane_base)
    if swap:
        out_ref = refs[0]
        refs[1][...] = unpack(jnp.sum(source_ref[:, width:, :], axis=0))
    else:
        fetch.wait()
    for l in range(sub_blocks):
        columns = slice(l * TILE, (l + 1) * TILE)
        piece = source_ref[l, :width, :] if swap else fetched[:, columns]
        source_parts[:width, columns], source_parts[width:, columns] = split(piece)

    def block(j, carry):
        lane_table[...] = lane_turns(j, sub_base, lane_base, sub_blocks, lane_poly)
        total = jnp.zeros((2 * width, 2 * TILE), f32)
        for l in range(0, sub_blocks, 2):
            lhs, rhs = [], []
            for at in (l, l + 1):
                columns = slice(at * TILE, (at + 1) * TILE)
                turn = sub_table[columns, :] + step_table[...] + lane_table[at:at + 1, :]
                rhs.append(jnp.concatenate(split(turn.astype(f32)), axis=1))
                listed = jnp.broadcast_to(mask_table[pl.ds(j * sub_blocks + at, 1), :], (2 * width, TILE)).astype(bf16)
                lhs.append(source_parts[:, columns] * listed)
            total += jnp.dot(
                jnp.concatenate(lhs, axis=1), jnp.concatenate(rhs, axis=0), preferred_element_type=f32
            )
        step_table[...] += growth_table[...]
        result = fold(total, scale / TURN)
        if swap:
            out_ref[:, pl.ds(pl.multiple_of(j * TILE, TILE), TILE)] = result
        else:
            out_ref[j] = result
        return carry

    lax.fori_loop(0, lane_blocks, block, 0, unroll=16)


SMEM, VMEM = pl.BlockSpec(memory_space=pltpu.SMEM), pl.BlockSpec(memory_space=pltpu.VMEM)


def cost(flops, traffic):
    return pl.CostEstimate(flops=flops, bytes_accessed=traffic, transcendentals=0)


def edge_product(base, count, pairs, source, lane_blocks, sub_blocks, swap, sub_poly, lane_poly, scale, width):
    out = jax.ShapeDtypeStruct((lane_blocks, width, TILE), f32)
    if swap:
        out = (
            jax.ShapeDtypeStruct((width, lane_blocks * TILE), f32),
            jax.ShapeDtypeStruct((2 * (source.shape[1] - width), TILE // 2), f32),
        )
    fetching = [] if swap else [pltpu.VMEM(source.shape, f32), pltpu.SemaphoreType.DMA]
    return pl.pallas_call(
        functools.partial(product_kernel, lane_blocks, sub_blocks, swap, sub_poly, lane_poly, scale, width),
        out_shape=out,
        in_specs=[SMEM, SMEM, VMEM, VMEM if swap else pl.BlockSpec(memory_space=pltpu.HBM)],
        out_specs=(VMEM, VMEM) if swap else VMEM,
        scratch_shapes=fetching + [
            pltpu.VMEM((sub_blocks * TILE, TILE), i32),
            pltpu.VMEM((TILE, TILE), i32),
            pltpu.VMEM((TILE, TILE), i32),
            pltpu.VMEM((sub_blocks, TILE), i32),
            pltpu.VMEM((lane_blocks * sub_blocks, TILE), f32),
            pltpu.VMEM((2 * width, sub_blocks * TILE), bf16),
        ],
        compiler_params=pltpu.CompilerParams(vmem_limit_bytes=(24 if swap else 60) << 20),
        cost_estimate=cost(8 << 30, 1 << 21),
    )(base, count, pairs, source)


def dot3(a, b):
    a_high, a_low = split(a)
    b_high, b_low = split(b)
    product = functools.partial(jnp.dot, preferred_element_type=f32)
    return product(a_high, b_high) + (product(a_high, b_low) + product(a_low, b_high))


def beside(values):
    return jnp.concatenate(values, axis=-1)


def layer_kernel(
    n_x, n_zh, at_ref, hidden_ref, own_ref, other_ref, both_ref,
    act_ref, grad_ref, own_terms_ref, other_terms_ref, weight,
):
    core, zh = at_ref[0], at_ref[1]
    half = own_ref.shape[0]
    packed, rows, width = own_terms_ref.shape[1], 2 * own_terms_ref.shape[1], own_ref.shape[2] // 2
    depth = hidden_ref.shape[0]
    for which, ref in ((core, own_ref), (1 - core, other_ref)):
        for z in range(0, n_zh, 2):
            pair = [ref[:, at * packed:(at + 1) * packed, :] for at in (z, z + 1)]
            wide = [beside([p[..., :width] for p in pair]), beside([p[..., width:] for p in pair])]
            wide = jnp.concatenate(wide, axis=1).reshape(half * rows, 2 * width)
            weight[pl.ds(pl.multiple_of(which * half * rows, 8), half * rows), z * width:(z + 2) * width] = wide
    cotangent = jnp.concatenate([both_ref[z, width + packed:, :] for z in range(n_zh)], axis=0).T

    pre = dot3(hidden_ref[...].T, weight[...])
    squash = 1.0 / (1.0 + jnp.exp(-pre))
    activations = (pre * squash).T
    grad_pre = cotangent * squash * (1.0 + pre * (1.0 - squash))
    n_rows = pre.shape[0]
    picked = [weight[pl.ds(pl.multiple_of((x * n_zh + zh) * width, 8), width), :] for x in range(n_x)]
    grad_ref[...] = dot3(jnp.concatenate(picked, axis=0), grad_pre.T).reshape(n_x, width, n_rows)

    for z in range(n_zh):
        columns = slice(z * width, (z + 1) * width)

        @pl.when(zh == z)
        def _():
            act_ref[...] = activations[columns, :]
            for which, ref in ((core, own_terms_ref), (1 - core, other_terms_ref)):
                part = hidden_ref[pl.ds(pl.multiple_of(which * (depth // 2), 8), depth // 2), :]
                ref[...] = pack(dot3(part, grad_pre[:, columns]).reshape(half, rows, width))


def layer(at, hidden_all, own, other, both, n_x, n_zh, rows):
    half = own.shape[0]
    width = own.shape[2] // 2
    n_rows = hidden_all.shape[1]
    terms = jax.ShapeDtypeStruct((half, rows // 2, 2 * width), f32)
    return pl.pallas_call(
        functools.partial(layer_kernel, n_x, n_zh),
        out_shape=(
            jax.ShapeDtypeStruct((width, n_rows), f32),
            jax.ShapeDtypeStruct((n_x, width, n_rows), f32),
            terms, terms,
        ),
        in_specs=[SMEM, VMEM, VMEM, VMEM, VMEM],
        out_specs=(VMEM, VMEM, VMEM, VMEM),
        scratch_shapes=[pltpu.VMEM((2 * half * rows, n_zh * width), f32)],
        compiler_params=pltpu.CompilerParams(vmem_limit_bytes=32 << 20),
        cost_estimate=cost(1 << 30, 1 << 21),
    )(at, hidden_all, own, other, both)


def copies(value, n):
    return jnp.broadcast_to(value[None], (n,) + value.shape)


def exchange(value, axes):
    return lax.all_to_all(value, axes, 0, 0)


def per_device(features, tile_list, tile_count, weight, cotangent):
    nbr, feat = ("zl", "y"), ("x", "zh")
    pairs, count = tile_list[0, 0], tile_count[0]
    n_nbr = lax.axis_size(nbr)
    n_x, n_zh = lax.axis_size("x"), lax.axis_size("zh")
    core, nbr_id = lax.axis_index("core"), lax.axis_index(nbr)
    width, c_dev = features.shape
    n_rows = cotangent.shape[0]
    r_dev = n_rows * n_nbr
    scale = (12.0 / (c_dev * n_nbr / 2)) ** 0.5
    row_blocks, col_blocks = r_dev // TILE, c_dev // TILE
    swap_core = [(0, 1), (1, 0)]

    rows_poly, cols_poly = (3, 11), (5, 13)
    packed = weight.shape[0] // 2
    bases = jnp.stack([nbr_id * c_dev, core * r_dev]).astype(i32)
    partial = edge_product(
        bases, count, pairs, features, row_blocks, col_blocks, False, cols_poly, rows_poly, scale, width
    )
    hidden = jnp.sum(exchange(partial, nbr), axis=0)
    gathered = lax.all_gather(jnp.concatenate([hidden, pack(weight), cotangent.T], axis=0), "zh")
    weight_z = gathered[:, width:width + packed].reshape(-1, TILE)
    hidden_z = gathered[:, :width].reshape(-1, n_rows)
    own = exchange(copies(weight_z, n_nbr), nbr)
    hidden_all = lax.all_gather(hidden_z, "x", axis=0, tiled=True)
    hidden_all, own = lax.optimization_barrier((hidden_all, own))
    other = lax.ppermute(own, "core", swap_core)

    at = jnp.stack([core, lax.axis_index("zh")]).astype(i32)
    activations, grad_terms, own_terms, other_terms = layer(
        at, hidden_all, own, other, gathered, n_x, n_zh, weight.shape[0]
    )
    other_terms = lax.ppermute(other_terms, "core", swap_core)
    grad_terms = exchange(grad_terms, "x")
    grad_hidden = copies(jnp.sum(grad_terms, axis=0), n_nbr)
    grad_block = exchange(jnp.concatenate([grad_hidden, own_terms + other_terms], axis=1), nbr)
    column_part, weight_grad = edge_product(
        bases[::-1], count, pairs, grad_block, col_blocks, row_blocks, True, rows_poly, cols_poly, scale, width
    )
    feature_grad = column_part + lax.ppermute(column_part, "core", swap_core)
    return activations.T, feature_grad, weight_grad


def halves(n):
    minor = 1
    while minor * minor < n:
        minor *= 2
    return n // minor, minor


def solution(mesh):
    sizes = (mesh.shape["row"], *halves(mesh.shape["nbr"]), *halves(mesh.shape["feat"]))
    fine = Mesh(mesh.devices.reshape(sizes), ("core", "zl", "y", "x", "zh"))
    nbr, feat = ("zl", "y"), ("x", "zh")
    rows = ("core", *nbr)
    in_specs = (P(feat, nbr), P("core", nbr, None, None), P("core", nbr), P(rows, feat), P(rows, feat))
    out_specs = (P(rows, feat), P(feat, nbr), P(rows, feat))
    return jax.shard_map(per_device, mesh=fine, in_specs=in_specs, out_specs=out_specs, check_vma=False)
```
